32 devices in a mesh: vert: 8 (over z, y), edge: 4 (over x, core).
Axes of the slice: x: 2, y: 2, z: 4, core: 2. Of those that a mesh axis runs over, the one named last changes fastest.
Arguments:
- features: float32 [16384, 256], P('vert'), may hold values from -6 to 6
- incidence: bfloat16 [64, 128, 512], P('vert', None, 'edge'), may hold values from 0 to 1, as said below
- send_count: int32 [64, 4], P('vert', 'edge'), may hold values from 0 to 1, as said below
- row_block: int32 [64, 4], P('vert', 'edge'), may hold values from 0 to 15
- edge_block: int32 [64, 4], P('vert', 'edge'), may hold values from 0 to 1
- edge_weight: float32 [16, 512], P('vert', 'edge'), may hold values from 0.25 to 4
- edge_degree: int32 [16, 512], P('vert', 'edge'), may hold values from 0 to 1024, as said below
- vertex_degree: int32 [16384], P('vert'), may hold values from 0 to 4096, as said below
Outputs:
- smoothed: float32 [16384, 256], P(('vert', 'edge'))
The draws below stay inside these ranges and needn't reach their ends.
Inputs may be any that keep to these rules, and one draw needn't show every extreme that they name: `incidence`: tile entries are 0 or 1. `send_count`: for each edge index one hyperedge block receives a live tile from every index of vert, in every draw. `edge_degree`: the column sums of H over live tiles; the most is reached in every draw. `vertex_degree`: the row sums of H over live tiles; the most is reached in every draw.
All inputs are finite; a program needn't handle non-finite values.
Results may differ from the reference program's by a relative error of at most 0.0049.
Values may be sent and summed in bfloat16 or wider, within the bound.
A program may use at most 64 MiB of HBM per device.

```python
import math
import jax
import jax.numpy as jnp
from jax import lax

ROWS_DEV = 2048
F = 256
BLOCK = 128
HB_DEV = 2
PAPERS = 16384
N_VERT = 8
N_EDGE = 4


def hyper_plan(key):
    base = jax.random.fold_in(key, 11)
    keys = jax.random.split(base, 7)
    vert_total = N_VERT
    edge_total = N_EDGE
    block_count = ROWS_DEV // BLOCK
    shape = (vert_total, vert_total, edge_total)
    send_live = (jax.random.randint(keys[0], shape, 0, 4) == 0).astype(jnp.int32)
    row_pick = jax.random.randint(keys[1], shape, 0, block_count).astype(jnp.int32)
    edge_pick = jax.random.randint(keys[2], shape, 0, HB_DEV).astype(jnp.int32)
    giant_owner = jax.random.randint(keys[3], (edge_total,), 0, vert_total)
    giant_block = jax.random.randint(keys[4], (edge_total,), 0, HB_DEV).astype(jnp.int32)
    is_giant = jnp.arange(vert_total)[None, :, None] == giant_owner[None, None, :]
    first_source = jnp.arange(vert_total)[:, None, None] == 0
    send_live = jnp.where(is_giant, 1, send_live).astype(jnp.int32)
    send_live = jnp.where(first_source, 1, send_live).astype(jnp.int32)
    row_pick = jnp.where(first_source, 0, row_pick).astype(jnp.int32)
    edge_pick = jnp.where(is_giant, giant_block[None, None, :], edge_pick).astype(jnp.int32)
    active = (jax.random.randint(keys[5], (vert_total, block_count, BLOCK), 0, 32) > 0).astype(jnp.int32)
    tile_bits = (jax.random.randint(keys[6], (vert_total, vert_total, BLOCK, edge_total, BLOCK), 0, 50) == 0).astype(jnp.int32)
    diagonal = (jnp.arange(BLOCK)[:, None] == jnp.arange(BLOCK)[None, :]).astype(jnp.int32)
    tile_bits = jnp.maximum(tile_bits, diagonal[None, None, :, None, :])
    row_active = active[jnp.arange(vert_total)[:, None, None], row_pick]
    tile_bits = tile_bits * jnp.transpose(row_active, (0, 1, 3, 2))[:, :, :, :, None]
    column_first = (jnp.arange(BLOCK) == 0)[None, None, None, None, :]
    giant_column = jnp.logical_and(jnp.broadcast_to(is_giant, shape)[:, :, None, :, None], column_first)
    tile_bits = jnp.maximum(tile_bits, giant_column.astype(jnp.int32))
    row_first = (jnp.arange(BLOCK) == 0)[None, None, :, None, None]
    full_row = jnp.logical_and(first_source[:, :, :, None, None], row_first)
    tile_bits = jnp.maximum(tile_bits, full_row.astype(jnp.int32))
    return (send_live, row_pick, edge_pick, tile_bits)


def draw_incidence(key, part):
    send_live, row_pick, edge_pick, tile_bits = hyper_plan(key)
    flat = tile_bits.reshape(N_VERT * N_VERT, BLOCK, N_EDGE * BLOCK)
    return flat.astype(jnp.float32).astype(jnp.bfloat16)


def draw_send_count(key, part):
    send_live, row_pick, edge_pick, tile_bits = hyper_plan(key)
    return send_live.reshape(N_VERT * N_VERT, N_EDGE)


def draw_row_block(key, part):
    send_live, row_pick, edge_pick, tile_bits = hyper_plan(key)
    return row_pick.reshape(N_VERT * N_VERT, N_EDGE)


def draw_edge_block(key, part):
    send_live, row_pick, edge_pick, tile_bits = hyper_plan(key)
    return edge_pick.reshape(N_VERT * N_VERT, N_EDGE)


def draw_edge_degree(key, part):
    send_live, row_pick, edge_pick, tile_bits = hyper_plan(key)
    live_bits = tile_bits * send_live[:, :, None, :, None]
    column_sums = jnp.sum(live_bits, axis=2)
    choose = (edge_pick[:, :, :, None] == jnp.arange(HB_DEV)[None, None, None, :]).astype(jnp.int32)
    degree = jnp.einsum('vdeh,vdeq->dheq', choose, column_sums)
    return degree.reshape(N_VERT * HB_DEV, N_EDGE * BLOCK).astype(jnp.int32)


def draw_vertex_degree(key, part):
    send_live, row_pick, edge_pick, tile_bits = hyper_plan(key)
    live_bits = tile_bits * send_live[:, :, None, :, None]
    row_sums = jnp.sum(live_bits, axis=4)
    choose = (row_pick[:, :, :, None] == jnp.arange(ROWS_DEV // BLOCK)[None, None, None, :]).astype(jnp.int32)
    degree = jnp.einsum('vdeb,vdpe->vbp', choose, row_sums)
    return degree.reshape(N_VERT * ROWS_DEV).astype(jnp.int32)


def levels(rng, shape, pieces, least, top_value):
    factor_of = 1.0
    for dim, parts in pieces:
        steps = jax.random.uniform(jax.random.fold_in(jax.random.fold_in(rng, 6), dim), (parts,), jnp.float32, least / len(pieces), top_value / len(pieces))
        factor_of = factor_of * jnp.repeat(jnp.exp(steps), shape[dim] // parts).reshape((-1,) + (1,) * (len(shape) - 1 - dim))
    return factor_of


def centred(rng, shape, scale, bound, cuts=(), dtype=jnp.bfloat16):
    level = levels(rng, shape, cuts, -0.22, 0.18) if cuts else 1.0
    drawn = jax.random.normal(rng, shape, jnp.float32) * scale * level
    return jnp.minimum(jnp.maximum(drawn, -bound), bound).astype(dtype)


def setup_inputs(seed: int = 0) -> dict:
    splits = jax.random.split(jax.random.key(seed), 9)
    return {
        "features": centred(splits[0], (PAPERS, F), 1.0, 6.0, ((0, 8),), jnp.float32),
        "incidence": draw_incidence(jax.random.fold_in(splits[8], 71), 0),
        "send_count": draw_send_count(jax.random.fold_in(splits[8], 71), 0),
        "row_block": draw_row_block(jax.random.fold_in(splits[8], 71), 0),
        "edge_block": draw_edge_block(jax.random.fold_in(splits[8], 71), 0),
        "edge_weight": jnp.clip(jnp.exp(math.log(4.0) - 2.7725887 * jax.random.uniform(splits[5], (N_VERT * HB_DEV, N_EDGE * BLOCK), jnp.float32) ** levels(splits[5], (N_VERT * HB_DEV, N_EDGE * BLOCK), ((0, 8), (1, 4)), -0.2, 0.2)), 0.25, 4.0),
        "edge_degree": draw_edge_degree(jax.random.fold_in(splits[8], 71), 0),
        "vertex_degree": draw_vertex_degree(jax.random.fold_in(splits[8], 71), 0),
    }


def reference(features, incidence, send_count, row_block, edge_block, edge_weight, edge_degree, vertex_degree):
    vert_total = N_VERT
    edge_total = N_EDGE
    block_count = ROWS_DEV // BLOCK
    tile_set = incidence.reshape(vert_total, vert_total, BLOCK, edge_total, BLOCK)
    live_slot = send_count.reshape(vert_total, vert_total, edge_total).astype(jnp.float32)
    row_index = row_block.reshape(vert_total, vert_total, edge_total)
    edge_index = edge_block.reshape(vert_total, vert_total, edge_total)
    row_scale = 1.0 / jnp.sqrt(jnp.maximum(vertex_degree, 1).astype(jnp.float32))
    row_scale = row_scale.reshape(vert_total, block_count, BLOCK, 1)
    hyper_scale = edge_weight / jnp.maximum(edge_degree, 1).astype(jnp.float32)
    hyper_scale = hyper_scale.reshape(vert_total, HB_DEV, edge_total, BLOCK, 1)
    owners = jnp.arange(vert_total)
    blocks = jnp.arange(block_count)
    hyper_ids = jnp.arange(HB_DEV)
    edge_ids = jnp.arange(edge_total)

    def apply_once(scaled_rows):

        def forward(total, source):
            tiles_here = tile_set[source].astype(jnp.float32)
            picked = scaled_rows[source][row_index[source]].astype(jnp.float32)
            partial_value = jnp.einsum('dpeq,depf->deqf', tiles_here, picked, precision=lax.Precision.HIGHEST)
            partial_value = (partial_value * live_slot[source][:, :, None, None]).astype(jnp.bfloat16).astype(jnp.float32)
            choose = (edge_index[source][:, :, None] == hyper_ids[None, None, :]).astype(jnp.float32)
            return (total + choose.transpose(0, 2, 1)[:, :, :, None, None] * partial_value[:, None], None)
        zero = jnp.zeros((vert_total, HB_DEV, edge_total, BLOCK, F), jnp.float32)
        summed, _ = lax.scan(forward, zero, owners)
        reply_all = (summed * hyper_scale).astype(jnp.bfloat16)

        def backward(source):
            reply = reply_all[owners[:, None], edge_index[source], edge_ids[None, :]].astype(jnp.float32)
            tiles_here = tile_set[source].astype(jnp.float32)
            spread = jnp.einsum('dpeq,deqf->dpef', tiles_here, reply, precision=lax.Precision.HIGHEST)
            choose = (row_index[source][None] == blocks[:, None, None]).astype(jnp.float32) * live_slot[source][None]
            return jnp.einsum('bde,dpef->bpf', choose, spread, precision=lax.Precision.HIGHEST)
        return lax.map(backward, owners)
    current = features.reshape(vert_total, block_count, BLOCK, F)
    for applied in range(2):
        scaled = (row_scale * current).astype(jnp.bfloat16)
        current = row_scale * apply_once(scaled)
    return current.reshape(vert_total * ROWS_DEV, F)
```

```python
import functools
import math

import jax
import jax.numpy as jnp
from jax import lax
from jax.experimental import pallas as pl
from jax.experimental.pallas import tpu as pltpu
from jax.sharding import PartitionSpec as P

MESH = pl.DeviceIdType.MESH
LANES = 128
BF16 = jnp.bfloat16
F32 = jnp.float32


def repeat(start, stop, body):
    if stop - start <= 8:
        for step in range(start, stop):
            body(step)
    else:

        @pl.loop(start, stop)
        def _(step):
            body(step)


def kernel(
    nv,
    ne,
    cols,
    feat,
    inc,
    live_s,
    row_s,
    edge_s,
    weight,
    degree,
    vdeg,
    out,
    tiles,
    meta_e,
    scale_e,
    meta_v,
    keys,
    owner_blocks,
    xs,
    rs,
    fwd_send,
    fwd_recv,
    bwd_send,
    bwd_recv,
    acc,
    prev,
    last,
    hyper_acc,
    hyper_feat,
    fin_send,
    fin_recv,
    meta_send_sem,
    meta_recv_sem,
    scale_send_sem,
    scale_recv_sem,
    tile_send_sem,
    tile_recv_sem,
    relay_sem,
    mv_send_sem,
    mv_recv_sem,
    fwd_send_sem,
    fwd_recv_sem,
    bwd_send_sem,
    bwd_recv_sem,
    fin_send_sem,
    fin_recv_sem,
    local_sem,
):
    v = lax.axis_index("vert")
    e = lax.axis_index("edge")
    block = inc.shape[1]
    blocks = xs.shape[0]
    hyper_blocks = weight.shape[0]
    share = blocks // ne
    none = nv * ne
    sibling = e + 1 - 2 * (e % 2)

    def edge_at(j):
        base = e + (j % 2) * (sibling - e)
        return (base + 2 * (j // 2)) % ne

    def to_edge(src, dst, send_sem, recv_sem, target):
        return pltpu.make_async_remote_copy(
            src_ref=src,
            dst_ref=dst,
            send_sem=send_sem,
            recv_sem=recv_sem,
            device_id=(v, target),
            device_id_type=MESH,
        )

    def to_vert(src, dst, send_sem, recv_sem, target):
        return pltpu.make_async_remote_copy(
            src_ref=src,
            dst_ref=dst,
            send_sem=send_sem,
            recv_sem=recv_sem,
            device_id=(target, e),
            device_id_type=MESH,
        )

    barrier = pltpu.get_barrier_semaphore()

    def greet_vert(t):
        pl.semaphore_signal(barrier, inc=1, device_id=((v + t) % nv, e), device_id_type=MESH)

    repeat(1, nv, greet_vert)
    for j in range(1, ne):
        pl.semaphore_signal(barrier, inc=1, device_id=(v, edge_at(j)), device_id_type=MESH)

    lane = lax.broadcasted_iota(jnp.int32, (8, LANES), 1)
    sub = lax.broadcasted_iota(jnp.int32, (8, LANES), 0)
    packed = jnp.zeros((8, LANES), jnp.int32)
    for s in range(nv):
        key = jnp.where(live_s[s, 0] > 0, row_s[s, 0], -1)
        both = jnp.where(sub == 0, key, edge_s[s, 0])
        packed = jnp.where(lane == s, both, packed)
    meta_e[e] = packed
    scale_e[e, :hyper_blocks] = weight[...] / jnp.maximum(degree[...], 1).astype(F32)

    pl.semaphore_wait(barrier, nv - 1 + ne - 1)

    meta_copies, tile_copies = [], []
    for j in range(1, ne):
        target = edge_at(j)
        meta_copies.append(
            to_edge(
                meta_e.at[e], meta_e.at[e], meta_send_sem.at[j], meta_recv_sem.at[e], target
            )
        )
        meta_copies.append(
            to_edge(
                scale_e.at[e], scale_e.at[e], scale_send_sem.at[j], scale_recv_sem.at[e], target
            )
        )
    for copy in meta_copies:
        copy.start()
    for j in [1] + list(range(2, ne, 2)):
        copy = to_edge(
            inc, tiles.at[e], tile_send_sem.at[j], tile_recv_sem.at[e], edge_at(j)
        )
        copy.start()
        tile_copies.append(copy)

    rs[...] = 1.0 / jnp.sqrt(jnp.maximum(vdeg[...], 1).astype(F32))
    group = LANES // cols
    start = pl.multiple_of((e // group) * LANES, LANES)
    part = e % group
    for b in range(blocks):
        turned = feat[pl.ds(b * block, block), pl.ds(start, LANES)].T
        picked = turned[:cols]
        for g in range(1, group):
            picked = jnp.where(part == g, turned[g * cols : (g + 1) * cols], picked)
        xs[b] = (picked * rs[b : b + 1, :]).astype(BF16)

    def tile_of(j, s):
        return inc[s] if j == 0 else tiles[edge_at(j), s]

    def partial(j, s):
        if j == 0:
            alive = live_s[s, 0] > 0
            row = row_s[s, 0]
        else:
            key = keys[edge_at(j), 0, s]
            alive = key >= 0
            row = jnp.maximum(key, 0)
        value = jnp.dot(xs[row], tile_of(j, s), preferred_element_type=F32)
        return jnp.where(alive, value, 0.0).astype(BF16)

    def fwd_copy(t):
        return to_vert(
            fwd_send.at[t],
            fwd_recv.at[v],
            fwd_send_sem.at[t],
            fwd_recv_sem.at[v],
            (v + t) % nv,
        )

    def fwd_arrival(source):
        return to_vert(
            fwd_send.at[0], fwd_recv.at[source], fwd_send_sem.at[0], fwd_recv_sem.at[source], v
        )

    def bwd_copy(t):
        return to_vert(
            bwd_send.at[t],
            bwd_recv.at[v],
            bwd_send_sem.at[t],
            bwd_recv_sem.at[v],
            (v + t) % nv,
        )

    def bwd_arrival(source):
        return to_vert(
            bwd_send.at[0], bwd_recv.at[source], bwd_send_sem.at[0], bwd_recv_sem.at[source], v
        )

    def mv_copy(t):
        return to_vert(
            meta_v.at[v], meta_v.at[v], mv_send_sem.at[t], mv_recv_sem.at[v], (v + t) % nv
        )

    def mv_arrival(source):
        return to_vert(
            meta_v.at[v], meta_v.at[source], mv_send_sem.at[0], mv_recv_sem.at[source], v
        )

    def tile_arrival(source):
        return to_edge(inc, tiles.at[source], tile_send_sem.at[0], tile_recv_sem.at[source], e)

    def first_part(j):
        here = edge_at(j)

        def step(t):
            fwd_send[t, here] = partial(j, (v + t) % nv)
            to_vert(
                fwd_send.at[t, here],
                fwd_recv.at[v, here],
                fwd_send_sem.at[t],
                fwd_recv_sem.at[v],
                (v + t) % nv,
            ).start()

        repeat(1, nv, step)
        fwd_recv[v, here] = partial(j, v)

    first_part(0)

    for j in range(1, ne):
        source = edge_at(j)
        to_edge(
            meta_e.at[e], meta_e.at[source], meta_send_sem.at[0], meta_recv_sem.at[source], e
        ).wait_recv()
        to_edge(
            scale_e.at[e], scale_e.at[source], scale_send_sem.at[0], scale_recv_sem.at[source], e
        ).wait_recv()
    to_scalars = pltpu.make_async_copy(meta_e, keys, local_sem.at[0])
    to_scalars.start()
    seen = jnp.zeros((8, LANES), jnp.int32)
    for other in range(ne):
        seen = jnp.where(sub == other, meta_e[other, 1:2, :], seen)
    meta_v[v] = seen
    repeat(1, nv, lambda t: mv_copy(t).start())
    to_scalars.wait()

    relays = []
    for j in range(1, ne):
        source = edge_at(j)
        tile_arrival(source).wait_recv()
        if j >= 2 and j % 2 == 0:
            copy = to_edge(
                tiles.at[source],
                tiles.at[source],
                relay_sem.at[j],
                tile_recv_sem.at[source],
                sibling,
            )
            copy.start()
            relays.append(copy)
        first_part(j)

    def link(i, latest):
        key = keys[edge_at(i % ne), 0, (v - i // ne + nv) % nv]
        before = none
        for b in range(blocks):
            before = jnp.where(key == b, latest[b], before)
        prev[i] = before
        return tuple(jnp.where(key == b, i, latest[b]) for b in range(blocks))

    latest = lax.fori_loop(0, none, link, (jnp.int32(none),) * blocks)
    for b in range(blocks):
        last[b] = latest[b]
    acc[none] = jnp.zeros(acc.shape[1:], F32)

    repeat(1, nv, lambda t: mv_arrival((v - t + nv) % nv).wait_recv())
    to_scalars = pltpu.make_async_copy(meta_v, owner_blocks, local_sem.at[1])
    to_scalars.start()
    to_scalars.wait()

    for applied in range(2):
        if applied:

            def send_all(t):
                for j in range(ne):
                    fwd_send[t, edge_at(j)] = partial(j, (v + t) % nv)
                fwd_copy(t).start()

            repeat(1, nv, send_all)
            for j in range(ne):
                fwd_recv[v, edge_at(j)] = partial(j, v)

        def add_from(source, first):
            for other in range(ne):
                held = owner_blocks[source, other, v]
                value = fwd_recv[source, other].astype(F32)
                for h in range(hyper_blocks):
                    term = jnp.where(held == h, value, 0.0)
                    hyper_acc[h, other] = term if first else hyper_acc[h, other] + term

        add_from(v, True)

        def arrive(t):
            source = (v - t + nv) % nv
            fwd_arrival(source).wait_recv()
            add_from(source, False)

        repeat(1, nv, arrive)
        for other in range(ne):
            for h in range(hyper_blocks):
                hyper_feat[h, other] = (
                    hyper_acc[h, other] * scale_e[other, h : h + 1, :]
                ).astype(BF16)

        def answer(t):
            if applied:
                bwd_copy(t).wait_send()
            for other in range(ne):
                held = owner_blocks[(v + t) % nv, other, v]
                bwd_send[t, other] = hyper_feat[held, other]
            bwd_copy(t).start()

        repeat(1, nv, answer)
        for other in range(ne):
            bwd_recv[v, other] = hyper_feat[owner_blocks[v, other, v], other]
        repeat(1, nv, lambda t: fwd_copy(t).wait_send())

        def spread(t):
            slot = (v - t + nv) % nv
            for j in range(ne):
                i = t * ne + j
                value = lax.dot_general(
                    bwd_recv[slot, edge_at(j)],
                    tile_of(j, slot),
                    (((1,), (1,)), ((), ())),
                    preferred_element_type=F32,
                )
                acc[i] = value + acc[prev[i]]

        spread(0)

        def come_back(t):
            bwd_arrival((v - t + nv) % nv).wait_recv()
            spread(t)

        repeat(1, nv, come_back)

        if applied == 0:
            for b in range(blocks):
                scale = rs[b : b + 1, :]
                xs[b] = (scale * (scale * acc[last[b]])).astype(BF16)

    fin_copies = []
    for j in range(ne - 1, -1, -1):
        target = edge_at(j)
        for k in range(share):
            b = target * share + k
            value = (rs[pl.ds(b, 1), :] * acc[last[b]]).astype(BF16)
            if j:
                fin_send[j, k] = value
            else:
                fin_recv[e, k] = value
        if j:
            copy = to_edge(
                fin_send.at[j], fin_recv.at[e], fin_send_sem.at[j], fin_recv_sem.at[e], target
            )
            copy.start()
            fin_copies.append(copy)
    for j in range(1, ne):
        source = edge_at(j)
        to_edge(
            fin_send.at[0], fin_recv.at[source], fin_send_sem.at[0], fin_recv_sem.at[source], e
        ).wait_recv()
    for k in range(share):
        for g in range(ne // group):
            stacked = jnp.concatenate(
                [fin_recv[g * group + i, k].astype(F32) for i in range(group)], axis=0
            )
            out[pl.ds(k * block, block), pl.ds(g * LANES, LANES)] = stacked.T

    for copy in meta_copies + tile_copies + relays + fin_copies:
        copy.wait_send()
    repeat(1, nv, lambda t: mv_copy(t).wait_send())
    repeat(1, nv, lambda t: bwd_copy(t).wait_send())


def shards(
    features, incidence, send_count, row_block, edge_block, edge_weight, edge_degree, vertex_degree
):
    nv = lax.axis_size("vert")
    ne = lax.axis_size("edge")
    papers, width = features.shape
    slots, block, _ = incidence.shape
    blocks = papers // block
    hyper_blocks = edge_weight.shape[0]
    cols = width // ne
    share = blocks // ne
    scratch = [
        ((ne, slots, block, block), BF16),
        ((ne, 8, LANES), jnp.int32),
        ((ne, 8, LANES), F32),
        ((nv, 8, LANES), jnp.int32),
        None,
        None,
        ((blocks, cols, block), BF16),
        ((blocks, block), F32),
        ((nv, ne, cols, block), BF16),
        ((nv, ne, cols, block), BF16),
        ((nv, ne, cols, block), BF16),
        ((nv, ne, cols, block), BF16),
        ((nv * ne + 1, cols, block), F32),
        None,
        None,
        ((hyper_blocks, ne, cols, block), F32),
        ((hyper_blocks, ne, cols, block), BF16),
        ((ne, share, cols, block), BF16),
        ((ne, share, cols, block), BF16),
    ]
    scalars = iter(
        [(ne, 8, LANES), (nv, 8, LANES), (nv * ne,), (blocks,)]
    )
    held = sum(
        math.prod(item[0]) * jnp.dtype(item[1]).itemsize for item in scratch if item is not None
    )
    held += features.size * 4 + incidence.size * 2 + papers // ne * width * 4
    shapes = [
        pltpu.SMEM(next(scalars), jnp.int32) if item is None else pltpu.VMEM(*item)
        for item in scratch
    ]
    dma = pltpu.SemaphoreType.DMA
    sems = [dma((ne,))] * 7 + [dma((nv,))] * 6 + [dma((ne,))] * 2 + [dma((2,))]
    vmem = pl.BlockSpec(memory_space=pltpu.VMEM)
    smem = pl.BlockSpec(memory_space=pltpu.SMEM)
    return pl.pallas_call(
        functools.partial(kernel, nv, ne, cols),
        out_shape=jax.ShapeDtypeStruct((papers // ne, width), F32),
        in_specs=[vmem, vmem, smem, smem, smem, vmem, vmem, vmem],
        out_specs=vmem,
        scratch_shapes=shapes + sems,
        compiler_params=pltpu.CompilerParams(
            collective_id=0,
            has_side_effects=True,
            vmem_limit_bytes=held + 6 * 2**20,
        ),
        cost_estimate=pl.CostEstimate(
            flops=8 * slots * ne * block * block * cols,
            bytes_accessed=features.size * 4 + incidence.size * 2,
            transcendentals=0,
        ),
    )(
        features,
        incidence,
        send_count,
        row_block,
        edge_block,
        edge_weight,
        edge_degree,
        vertex_degree.reshape(blocks, block),
    )


def solution(mesh):
    placed = (
        P("vert", None),
        P("vert", None, "edge"),
        P("vert", "edge"),
        P("vert", "edge"),
        P("vert", "edge"),
        P("vert", "edge"),
        P("vert", "edge"),
        P("vert"),
    )
    return jax.shard_map(
        shards, mesh=mesh, in_specs=placed, out_specs=P(("vert", "edge"), None), check_vma=False
    )
```

```python
import functools
import math

import jax
import jax.numpy as jnp
from jax import lax
from jax.experimental import pallas as pl
from jax.experimental.pallas import tpu as pltpu
from jax.sharding import PartitionSpec as P

MESH = pl.DeviceIdType.MESH
LANES = 128
BF16 = jnp.bfloat16
F32 = jnp.float32


def repeat(start, stop, body):
    if stop - start <= 8:
        for step in range(start, stop):
            body(step)
    else:

        @pl.loop(start, stop)
        def _(step):
            body(step)


def kernel(
    nv,
    ne,
    chunks,
    feat,
    inc,
    live_s,
    row_s,
    edge_s,
    weight,
    degree,
    vdeg,
    out,
    mine,
    weight_v,
    degree_v,
    vdeg_v,
    tiles,
    meta_e,
    scale_e,
    meta_v,
    keys,
    owner_blocks,
    xs,
    rs,
    fwd_send,
    fwd_recv,
    bwd_send,
    bwd_recv,
    acc,
    prev,
    last,
    hyper_acc,
    hyper_feat,
    fin_send,
    fin_recv,
    meta_send_sem,
    meta_recv_sem,
    scale_send_sem,
    scale_recv_sem,
    tile_send_sem,
    tile_recv_sem,
    relay_sem,
    mv_send_sem,
    mv_recv_sem,
    fwd_send_sem,
    fwd_recv_sem,
    bwd_send_sem,
    bwd_recv_sem,
    fin_send_sem,
    fin_recv_sem,
    local_sem,
):
    v = lax.axis_index("vert")
    e = lax.axis_index("edge")
    block = inc.shape[1]
    blocks = xs.shape[1]
    part_cols = xs.shape[2]
    cols = chunks * part_cols
    hyper_blocks = weight.shape[0]
    share = blocks // ne
    none = nv * ne
    sibling = e + 1 - 2 * (e % 2)

    def edge_at(j):
        base = e + (j % 2) * (sibling - e)
        return (base + 2 * (j // 2)) % ne

    def pair_at(m):
        return pl.ds((e - e % 2 + 2 * m) % ne, 2)

    def to_edge(src, dst, send_sem, recv_sem, target):
        return pltpu.make_async_remote_copy(
            src_ref=src,
            dst_ref=dst,
            send_sem=send_sem,
            recv_sem=recv_sem,
            device_id=(v, target),
            device_id_type=MESH,
        )

    def to_vert(src, dst, send_sem, recv_sem, target):
        return pltpu.make_async_remote_copy(
            src_ref=src,
            dst_ref=dst,
            send_sem=send_sem,
            recv_sem=recv_sem,
            device_id=(target, e),
            device_id_type=MESH,
        )

    group = LANES // cols
    start = pl.multiple_of((e // group) * LANES, LANES)
    part = e % group
    fetches = [
        pltpu.make_async_copy(weight, weight_v, local_sem.at[2]),
        pltpu.make_async_copy(degree, degree_v, local_sem.at[3]),
        pltpu.make_async_copy(vdeg, vdeg_v, local_sem.at[4]),
        pltpu.make_async_copy(feat.at[:, pl.ds(start, LANES)], mine, local_sem.at[5]),
        pltpu.make_async_copy(inc, tiles.at[e], local_sem.at[6]),
    ]
    for copy in fetches:
        copy.start()

    barrier = pltpu.get_barrier_semaphore()

    def greet_vert(t):
        pl.semaphore_signal(barrier, inc=1, device_id=((v + t) % nv, e), device_id_type=MESH)

    repeat(1, nv, greet_vert)
    for j in range(1, ne):
        pl.semaphore_signal(barrier, inc=1, device_id=(v, edge_at(j)), device_id_type=MESH)

    lane = lax.broadcasted_iota(jnp.int32, (8, LANES), 1)
    sub = lax.broadcasted_iota(jnp.int32, (8, LANES), 0)
    packed = jnp.zeros((8, LANES), jnp.int32)
    for s in range(nv):
        key = jnp.where(live_s[0, s] > 0, row_s[0, s], -1)
        both = jnp.where(sub == 0, key, edge_s[0, s])
        packed = jnp.where(lane == s, both, packed)
    meta_e[e] = packed
    for copy in fetches[:2]:
        copy.wait()
    scale_e[e, :hyper_blocks] = weight_v[...] / jnp.maximum(degree_v[...], 1).astype(F32)

    pl.semaphore_wait(barrier, nv - 1 + ne - 1)

    meta_copies, tile_copies = [], []
    for j in range(1, ne):
        target = edge_at(j)
        meta_copies.append(
            to_edge(
                meta_e.at[e], meta_e.at[e], meta_send_sem.at[j], meta_recv_sem.at[e], target
            )
        )
        meta_copies.append(
            to_edge(
                scale_e.at[e], scale_e.at[e], scale_send_sem.at[j], scale_recv_sem.at[e], target
            )
        )
    for copy in meta_copies:
        copy.start()
    for j in [1] + list(range(2, ne, 2)):
        copy = to_edge(
            inc, tiles.at[e], tile_send_sem.at[j], tile_recv_sem.at[e], edge_at(j)
        )
        copy.start()
        tile_copies.append(copy)

    for copy in fetches[2:4]:
        copy.wait()
    rs[...] = 1.0 / jnp.sqrt(jnp.maximum(vdeg_v[...], 1).astype(F32))
    for b in range(blocks):
        turned = mine[pl.ds(b * block, block), :].T
        picked = turned[:cols]
        for g in range(1, group):
            picked = jnp.where(part == g, turned[g * cols : (g + 1) * cols], picked)
        picked = (picked * rs[b : b + 1, :]).astype(BF16)
        for c in range(chunks):
            xs[c, b] = picked[c * part_cols : (c + 1) * part_cols]
    fetches[4].wait()

    def slot_of(j, s):
        if j == 0:
            return live_s[0, s] > 0, row_s[0, s]
        key = keys[edge_at(j), 0, s]
        return key >= 0, jnp.maximum(key, 0)

    def partial(j, s, some):
        alive, row = slot_of(j, s)
        held = [xs[c, row] for c in some]
        left = held[0] if len(held) == 1 else jnp.concatenate(held, axis=0)
        value = jnp.dot(left, tiles[edge_at(j), s], preferred_element_type=F32)
        return jnp.where(alive, value, 0.0).astype(BF16)

    def fwd_copy(c, t):
        return to_vert(
            fwd_send.at[c, t],
            fwd_recv.at[c, v],
            fwd_send_sem.at[c, t],
            fwd_recv_sem.at[c, v],
            (v + t) % nv,
        )

    def fwd_arrival(c, source):
        return to_vert(
            fwd_send.at[c, 0],
            fwd_recv.at[c, source],
            fwd_send_sem.at[c, 0],
            fwd_recv_sem.at[c, source],
            v,
        )

    def bwd_copy(c, t):
        return to_vert(
            bwd_send.at[c, t],
            bwd_recv.at[c, v],
            bwd_send_sem.at[c, t],
            bwd_recv_sem.at[c, v],
            (v + t) % nv,
        )

    def bwd_arrival(c, source):
        return to_vert(
            bwd_send.at[c, 0],
            bwd_recv.at[c, source],
            bwd_send_sem.at[c, 0],
            bwd_recv_sem.at[c, source],
            v,
        )

    def mv_copy(t):
        return to_vert(
            meta_v.at[v], meta_v.at[v], mv_send_sem.at[t], mv_recv_sem.at[v], (v + t) % nv
        )

    def mv_arrival(source):
        return to_vert(
            meta_v.at[v], meta_v.at[source], mv_send_sem.at[0], mv_recv_sem.at[source], v
        )

    def tile_arrival(source):
        return to_edge(inc, tiles.at[source], tile_send_sem.at[0], tile_recv_sem.at[source], e)

    def first_part(j):
        here = edge_at(j)

        def step(t):
            value = partial(j, (v + t) % nv, range(chunks))
            for c in range(chunks):
                fwd_send[c, t, here] = value[c * part_cols : (c + 1) * part_cols]

        repeat(1, nv, step)
        value = partial(j, v, range(chunks))
        for c in range(chunks):
            fwd_recv[c, v, here] = value[c * part_cols : (c + 1) * part_cols]

    def first_pair(m):
        pair = pair_at(m)

        for c in range(chunks):

            def step(t):
                to_vert(
                    fwd_send.at[c, t, pair],
                    fwd_recv.at[c, v, pair],
                    fwd_send_sem.at[c, t],
                    fwd_recv_sem.at[c, v],
                    (v + t) % nv,
                ).start()

            repeat(1, nv, step)

    first_part(0)

    for j in range(1, ne):
        source = edge_at(j)
        to_edge(
            meta_e.at[e], meta_e.at[source], meta_send_sem.at[0], meta_recv_sem.at[source], e
        ).wait_recv()
        to_edge(
            scale_e.at[e], scale_e.at[source], scale_send_sem.at[0], scale_recv_sem.at[source], e
        ).wait_recv()
    to_scalars = pltpu.make_async_copy(meta_e, keys, local_sem.at[0])
    to_scalars.start()
    seen = jnp.zeros((8, LANES), jnp.int32)
    for other in range(ne):
        seen = jnp.where(sub == other, meta_e[other, 1:2, :], seen)
    meta_v[v] = seen
    repeat(1, nv, lambda t: mv_copy(t).start())
    to_scalars.wait()

    relays = []
    for j in range(1, ne):
        source = edge_at(j)
        tile_arrival(source).wait_recv()
        if j >= 2 and j % 2 == 0:
            copy = to_edge(
                tiles.at[source],
                tiles.at[source],
                relay_sem.at[j],
                tile_recv_sem.at[source],
                sibling,
            )
            copy.start()
            relays.append(copy)
        first_part(j)
        if j % 2:
            first_pair(j // 2)

    def link(i, latest):
        key = keys[edge_at(i % ne), 0, (v - i // ne + nv) % nv]
        before = none
        for b in range(blocks):
            before = jnp.where(key == b, latest[b], before)
        prev[i] = before
        return tuple(jnp.where(key == b, i, latest[b]) for b in range(blocks))

    latest = lax.fori_loop(0, none, link, (jnp.int32(none),) * blocks)
    for b in range(blocks):
        last[b] = latest[b]
    for c in range(chunks):
        acc[c, none] = jnp.zeros(acc.shape[2:], F32)

    repeat(1, nv, lambda t: mv_arrival((v - t + nv) % nv).wait_recv())
    to_scalars = pltpu.make_async_copy(meta_v, owner_blocks, local_sem.at[1])
    to_scalars.start()
    to_scalars.wait()

    def send_again(c):
        def send_all(t):
            for j in range(ne):
                fwd_send[c, t, edge_at(j)] = partial(j, (v + t) % nv, (c,))
            fwd_copy(c, t).start()

        repeat(1, nv, send_all)
        for j in range(ne):
            fwd_recv[c, v, edge_at(j)] = partial(j, v, (c,))

    def answer_all(c, applied):
        def add_from(source, first):
            for other in range(ne):
                held = owner_blocks[source, other, v]
                value = fwd_recv[c, source, other].astype(F32)
                for h in range(hyper_blocks):
                    term = jnp.where(held == h, value, 0.0)
                    hyper_acc[h, other] = term if first else hyper_acc[h, other] + term

        add_from(v, True)

        def arrive(t):
            source = (v - t + nv) % nv
            fwd_arrival(c, source).wait_recv()
            add_from(source, False)

        repeat(1, nv, arrive)
        for other in range(ne):
            for h in range(hyper_blocks):
                hyper_feat[h, other] = (
                    hyper_acc[h, other] * scale_e[other, h : h + 1, :]
                ).astype(BF16)

        def answer(t):
            if applied:
                bwd_copy(c, t).wait_send()
            for other in range(ne):
                held = owner_blocks[(v + t) % nv, other, v]
                bwd_send[c, t, other] = hyper_feat[held, other]
            bwd_copy(c, t).start()

        repeat(1, nv, answer)
        for other in range(ne):
            bwd_recv[c, v, other] = hyper_feat[owner_blocks[v, other, v], other]
        repeat(1, nv, lambda t: fwd_copy(c, t).wait_send())

    def gather_rows(c):
        def spread(t):
            slot = (v - t + nv) % nv
            for j in range(ne):
                i = t * ne + j
                value = lax.dot_general(
                    bwd_recv[c, slot, edge_at(j)],
                    tiles[edge_at(j), slot],
                    (((1,), (1,)), ((), ())),
                    preferred_element_type=F32,
                )
                acc[c, i] = value + acc[c, prev[i]]

        spread(0)

        def come_back(t):
            bwd_arrival(c, (v - t + nv) % nv).wait_recv()
            spread(t)

        repeat(1, nv, come_back)

    def fin_copy(c, j):
        return to_edge(
            fin_send.at[c, j],
            fin_recv.at[c, e],
            fin_send_sem.at[c, j],
            fin_recv_sem.at[c, e],
            edge_at(j),
        )

    def finish(c):
        for j in range(ne - 1, -1, -1):
            for k in range(share):
                b = edge_at(j) * share + k
                value = (rs[pl.ds(b, 1), :] * acc[c, last[b]]).astype(BF16)
                if j:
                    fin_send[c, j, k] = value
                else:
                    fin_recv[c, e, k] = value
            if j:
                fin_copy(c, j).start()

    for applied in range(2):
        for c in range(chunks):
            answer_all(c, applied)
        for c in range(chunks):
            gather_rows(c)
            if applied:
                finish(c)
            else:
                for b in range(blocks):
                    scale = rs[b : b + 1, :]
                    xs[c, b] = (scale * (scale * acc[c, last[b]])).astype(BF16)
                send_again(c)

    for c in range(chunks):
        for j in range(1, ne):
            source = edge_at(j)
            to_edge(
                fin_send.at[c, 0],
                fin_recv.at[c, source],
                fin_send_sem.at[c, 0],
                fin_recv_sem.at[c, source],
                e,
            ).wait_recv()
    for k in range(share):
        for g in range(ne // group):
            stacked = jnp.concatenate(
                [
                    fin_recv[c, g * group + i, k].astype(F32)
                    for i in range(group)
                    for c in range(chunks)
                ],
                axis=0,
            )
            out[pl.ds(k * block, block), pl.ds(g * LANES, LANES)] = stacked.T

    for copy in meta_copies + tile_copies + relays:
        copy.wait_send()
    repeat(1, nv, lambda t: mv_copy(t).wait_send())
    for c in range(chunks):
        repeat(1, nv, lambda t: bwd_copy(c, t).wait_send())
        for j in range(1, ne):
            fin_copy(c, j).wait_send()


def shards(
    features, incidence, send_count, row_block, edge_block, edge_weight, edge_degree, vertex_degree
):
    nv = lax.axis_size("vert")
    ne = lax.axis_size("edge")
    papers, width = features.shape
    slots, block, _ = incidence.shape
    blocks = papers // block
    hyper_blocks = edge_weight.shape[0]
    cols = width // ne
    share = blocks // ne
    chunks = max(1, cols // 32)
    cut = cols // chunks
    scratch = [
        ((papers, LANES), F32),
        ((hyper_blocks, block), F32),
        ((hyper_blocks, block), jnp.int32),
        ((blocks, block), jnp.int32),
        ((ne, slots, block, block), BF16),
        ((ne, 8, LANES), jnp.int32),
        ((ne, 8, LANES), F32),
        ((nv, 8, LANES), jnp.int32),
        None,
        None,
        ((chunks, blocks, cut, block), BF16),
        ((blocks, block), F32),
        ((chunks, nv, ne, cut, block), BF16),
        ((chunks, nv, ne, cut, block), BF16),
        ((chunks, nv, ne, cut, block), BF16),
        ((chunks, nv, ne, cut, block), BF16),
        ((chunks, nv * ne + 1, cut, block), F32),
        None,
        None,
        ((hyper_blocks, ne, cut, block), F32),
        ((hyper_blocks, ne, cut, block), BF16),
        ((chunks, ne, share, cut, block), BF16),
        ((chunks, ne, share, cut, block), BF16),
    ]
    scalars = iter(
        [(ne, 8, LANES), (nv, 8, LANES), (nv * ne,), (blocks,)]
    )
    held = sum(
        math.prod(item[0]) * jnp.dtype(item[1]).itemsize for item in scratch if item is not None
    )
    held += papers // ne * width * 4
    shapes = [
        pltpu.SMEM(next(scalars), jnp.int32) if item is None else pltpu.VMEM(*item)
        for item in scratch
    ]
    dma = pltpu.SemaphoreType.DMA
    sems = [dma((ne,))] * 7 + [dma((nv,))] * 2 + [dma((chunks, nv))] * 4
    sems += [dma((chunks, ne))] * 2 + [dma((7,))]
    hbm = pl.BlockSpec(memory_space=pltpu.HBM)
    vmem = pl.BlockSpec(memory_space=pltpu.VMEM)
    smem = pl.BlockSpec(memory_space=pltpu.SMEM)
    return pl.pallas_call(
        functools.partial(kernel, nv, ne, chunks),
        out_shape=jax.ShapeDtypeStruct((papers // ne, width), F32),
        in_specs=[hbm, hbm, smem, smem, smem, hbm, hbm, hbm],
        out_specs=vmem,
        scratch_shapes=shapes + sems,
        compiler_params=pltpu.CompilerParams(
            collective_id=0,
            has_side_effects=True,
            vmem_limit_bytes=max(held + 6 * 2**20, 60 * 2**20),
        ),
        cost_estimate=pl.CostEstimate(
            flops=8 * slots * ne * block * block * cols,
            bytes_accessed=features.size * 4 + incidence.size * 2,
            transcendentals=0,
        ),
    )(
        features,
        incidence,
        send_count.reshape(1, slots),
        row_block.reshape(1, slots),
        edge_block.reshape(1, slots),
        edge_weight,
        edge_degree,
        vertex_degree.reshape(blocks, block),
    )


def solution(mesh):
    placed = (
        P("vert", None),
        P("vert", None, "edge"),
        P("vert", "edge"),
        P("vert", "edge"),
        P("vert", "edge"),
        P("vert", "edge"),
        P("vert", "edge"),
        P("vert"),
    )
    return jax.shard_map(
        shards, mesh=mesh, in_specs=placed, out_specs=P(("vert", "edge"), None), check_vma=False
    )
```

```python
import functools
import math

import jax
import jax.numpy as jnp
from jax import lax
from jax.experimental import pallas as pl
from jax.experimental.pallas import tpu as pltpu
from jax.sharding import PartitionSpec as P

MESH = pl.DeviceIdType.MESH
LANES = 128
BF16 = jnp.bfloat16
F32 = jnp.float32


def repeat(start, stop, body):
    if stop - start <= 8:
        for step in range(start, stop):
            body(step)
    else:

        @pl.loop(start, stop)
        def _(step):
            body(step)


def kernel(
    nv,
    ne,
    chunks,
    feat,
    inc,
    live_s,
    row_s,
    edge_s,
    weight,
    degree,
    vdeg,
    out,
    mine,
    weight_v,
    degree_v,
    vdeg_v,
    tiles,
    meta_e,
    scale_e,
    scale_m,
    meta_v,
    keys,
    owner_blocks,
    xs,
    rs,
    fwd_send,
    fwd_recv,
    bwd_send,
    bwd_recv,
    acc,
    prev,
    last,
    hyper_acc,
    hyper_feat,
    mir_send,
    mir_recv,
    fin_send,
    fin_recv,
    meta_send_sem,
    meta_recv_sem,
    scale_send_sem,
    scale_recv_sem,
    tile_send_sem,
    tile_recv_sem,
    relay_sem,
    mv_send_sem,
    mv_recv_sem,
    fwd_send_sem,
    fwd_recv_sem,
    bwd_send_sem,
    bwd_recv_sem,
    fin_send_sem,
    fin_recv_sem,
    mir_send_sem,
    mir_recv_sem,
    local_sem,
):
    v = lax.axis_index("vert")
    e = lax.axis_index("edge")
    block = inc.shape[1]
    blocks = xs.shape[1]
    part_cols = xs.shape[2]
    cols = chunks * part_cols
    hyper_blocks = weight.shape[0]
    share = blocks // ne
    none = nv * ne
    half = nv // 2
    here = v % half
    base = v - here
    mirror = (v + half) % nv
    sibling = e + 1 - 2 * (e % 2)

    def edge_at(j):
        first = e + (j % 2) * (sibling - e)
        return (first + 2 * (j // 2)) % ne

    def pair_at(m):
        return pl.ds((e - e % 2 + 2 * m) % ne, 2)

    def ahead(t):
        return base + (here + t) % half

    def behind(t):
        return (here - t + half) % half

    def to_edge(src, dst, send_sem, recv_sem, target):
        return pltpu.make_async_remote_copy(
            src_ref=src,
            dst_ref=dst,
            send_sem=send_sem,
            recv_sem=recv_sem,
            device_id=(v, target),
            device_id_type=MESH,
        )

    def to_vert(src, dst, send_sem, recv_sem, target):
        return pltpu.make_async_remote_copy(
            src_ref=src,
            dst_ref=dst,
            send_sem=send_sem,
            recv_sem=recv_sem,
            device_id=(target, e),
            device_id_type=MESH,
        )

    group = LANES // cols
    start = pl.multiple_of((e // group) * LANES, LANES)
    part = e % group
    fetches = [
        pltpu.make_async_copy(weight, weight_v, local_sem.at[2]),
        pltpu.make_async_copy(degree, degree_v, local_sem.at[3]),
        pltpu.make_async_copy(vdeg, vdeg_v, local_sem.at[4]),
        pltpu.make_async_copy(feat.at[:, pl.ds(start, LANES)], mine, local_sem.at[5]),
        pltpu.make_async_copy(inc, tiles.at[e], local_sem.at[6]),
    ]
    for copy in fetches:
        copy.start()

    barrier = pltpu.get_barrier_semaphore()

    def greet_vert(t):
        pl.semaphore_signal(barrier, inc=1, device_id=(ahead(t), e), device_id_type=MESH)

    repeat(1, half, greet_vert)
    pl.semaphore_signal(barrier, inc=1, device_id=(mirror, e), device_id_type=MESH)
    for j in range(1, ne):
        pl.semaphore_signal(barrier, inc=1, device_id=(v, edge_at(j)), device_id_type=MESH)

    lane = lax.broadcasted_iota(jnp.int32, (8, LANES), 1)
    sub = lax.broadcasted_iota(jnp.int32, (8, LANES), 0)
    packed = jnp.zeros((8, LANES), jnp.int32)
    for s in range(nv):
        key = jnp.where(live_s[0, s] > 0, row_s[0, s], -1)
        both = jnp.where(sub == 0, key, edge_s[0, s])
        packed = jnp.where(lane == s, both, packed)
    meta_e[e] = packed
    for copy in fetches[:2]:
        copy.wait()
    scale_e[e, :hyper_blocks] = weight_v[...] / jnp.maximum(degree_v[...], 1).astype(F32)

    pl.semaphore_wait(barrier, half + ne - 1)

    meta_copies, tile_copies = [], []
    for j in range(1, ne):
        target = edge_at(j)
        meta_copies.append(
            to_edge(
                meta_e.at[e], meta_e.at[e], meta_send_sem.at[j], meta_recv_sem.at[e], target
            )
        )
        meta_copies.append(
            to_edge(
                scale_e.at[e], scale_e.at[e], scale_send_sem.at[j], scale_recv_sem.at[e], target
            )
        )
    for copy in meta_copies:
        copy.start()
    for j in [1] + list(range(2, ne, 2)):
        copy = to_edge(
            inc, tiles.at[e], tile_send_sem.at[j], tile_recv_sem.at[e], edge_at(j)
        )
        copy.start()
        tile_copies.append(copy)

    for copy in fetches[2:4]:
        copy.wait()
    rs[...] = 1.0 / jnp.sqrt(jnp.maximum(vdeg_v[...], 1).astype(F32))
    for b in range(blocks):
        turned = mine[pl.ds(b * block, block), :].T
        picked = turned[:cols]
        for g in range(1, group):
            picked = jnp.where(part == g, turned[g * cols : (g + 1) * cols], picked)
        picked = (picked * rs[b : b + 1, :]).astype(BF16)
        for c in range(chunks):
            xs[c, b] = picked[c * part_cols : (c + 1) * part_cols]
    fetches[4].wait()

    def slot_of(j, s):
        if j == 0:
            return live_s[0, s] > 0, row_s[0, s]
        key = keys[edge_at(j), 0, s]
        return key >= 0, jnp.maximum(key, 0)

    def partial(j, s, some):
        alive, row = slot_of(j, s)
        held = [xs[c, row] for c in some]
        left = held[0] if len(held) == 1 else jnp.concatenate(held, axis=0)
        value = jnp.dot(left, tiles[edge_at(j), s], preferred_element_type=F32)
        return jnp.where(alive, value, 0.0).astype(BF16)

    def fwd_copy(c, t):
        return to_vert(
            fwd_send.at[c, t],
            fwd_recv.at[c, here],
            fwd_send_sem.at[c, t],
            fwd_recv_sem.at[c, here],
            ahead(t),
        )

    def fwd_arrival(c, source):
        return to_vert(
            fwd_send.at[c, 0],
            fwd_recv.at[c, source],
            fwd_send_sem.at[c, 0],
            fwd_recv_sem.at[c, source],
            v,
        )

    def bwd_copy(c, t):
        return to_vert(
            bwd_send.at[c, t],
            bwd_recv.at[c, here],
            bwd_send_sem.at[c, t],
            bwd_recv_sem.at[c, here],
            ahead(t),
        )

    def bwd_arrival(c, source):
        return to_vert(
            bwd_send.at[c, 0],
            bwd_recv.at[c, source],
            bwd_send_sem.at[c, 0],
            bwd_recv_sem.at[c, source],
            v,
        )

    def mv_copy(t):
        return to_vert(
            meta_v.at[here], meta_v.at[here], mv_send_sem.at[t], mv_recv_sem.at[here], ahead(t)
        )

    def mv_arrival(source):
        return to_vert(
            meta_v.at[here], meta_v.at[source], mv_send_sem.at[0], mv_recv_sem.at[source], v
        )

    def tile_arrival(source):
        return to_edge(inc, tiles.at[source], tile_send_sem.at[0], tile_recv_sem.at[source], e)

    def mir_copy(p):
        return to_vert(
            mir_send.at[p], mir_recv.at[p], mir_send_sem.at[p], mir_recv_sem.at[p], mirror
        )

    scale_copy = to_vert(
        scale_e, scale_m, mir_send_sem.at[2 * chunks], mir_recv_sem.at[2 * chunks], mirror
    )

    def first_part(j):
        other = edge_at(j)

        def step(t):
            for q in range(2):
                value = partial(j, q * half + (here + t) % half, range(chunks))
                for c in range(chunks):
                    fwd_send[c, t, other, q] = value[c * part_cols : (c + 1) * part_cols]

        repeat(1, half, step)
        for q in range(2):
            value = partial(j, q * half + here, range(chunks))
            for c in range(chunks):
                fwd_recv[c, here, other, q] = value[c * part_cols : (c + 1) * part_cols]

    def first_pair(m):
        pair = pair_at(m)

        for c in range(chunks):

            def step(t):
                to_vert(
                    fwd_send.at[c, t, pair],
                    fwd_recv.at[c, here, pair],
                    fwd_send_sem.at[c, t],
                    fwd_recv_sem.at[c, here],
                    ahead(t),
                ).start()

            repeat(1, half, step)

    first_part(0)

    for j in range(1, ne):
        source = edge_at(j)
        to_edge(
            meta_e.at[e], meta_e.at[source], meta_send_sem.at[0], meta_recv_sem.at[source], e
        ).wait_recv()
        to_edge(
            scale_e.at[e], scale_e.at[source], scale_send_sem.at[0], scale_recv_sem.at[source], e
        ).wait_recv()
    to_scalars = pltpu.make_async_copy(meta_e, keys, local_sem.at[0])
    to_scalars.start()
    seen = jnp.zeros((8, LANES), jnp.int32)
    for other in range(ne):
        seen = jnp.where(sub == other, meta_e[other, 1:2, :], seen)
    meta_v[here] = seen
    repeat(1, half, lambda t: mv_copy(t).start())
    scale_copy.start()
    to_scalars.wait()

    relays = []
    for j in range(1, ne):
        source = edge_at(j)
        tile_arrival(source).wait_recv()
        if j >= 2 and j % 2 == 0:
            copy = to_edge(
                tiles.at[source],
                tiles.at[source],
                relay_sem.at[j],
                tile_recv_sem.at[source],
                sibling,
            )
            copy.start()
            relays.append(copy)
        first_part(j)
        if j % 2:
            first_pair(j // 2)

    def link(i, latest):
        slot = ((i // ne) % 2) * half + behind(i // (2 * ne))
        key = keys[edge_at(i % ne), 0, slot]
        before = none
        for b in range(blocks):
            before = jnp.where(key == b, latest[b], before)
        prev[i] = before
        return tuple(jnp.where(key == b, i, latest[b]) for b in range(blocks))

    latest = lax.fori_loop(0, none, link, (jnp.int32(none),) * blocks)
    for b in range(blocks):
        last[b] = latest[b]
    for c in range(chunks):
        acc[c, none] = jnp.zeros(acc.shape[2:], F32)

    repeat(1, half, lambda t: mv_arrival(behind(t)).wait_recv())
    to_scalars = pltpu.make_async_copy(meta_v, owner_blocks, local_sem.at[1])
    to_scalars.start()
    to_scalars.wait()

    def send_again(c):
        def send_all(t):
            for j in range(ne):
                for q in range(2):
                    slot = q * half + (here + t) % half
                    fwd_send[c, t, edge_at(j), q] = partial(j, slot, (c,))
            fwd_copy(c, t).start()

        repeat(1, half, send_all)
        for j in range(ne):
            for q in range(2):
                fwd_recv[c, here, edge_at(j), q] = partial(j, q * half + here, (c,))

    def sum_half(c, applied):
        def add_from(source, first):
            for other in range(ne):
                for q in range(2):
                    held = owner_blocks[source, other, q * half + here]
                    value = fwd_recv[c, source, other, q].astype(F32)
                    for h in range(hyper_blocks):
                        term = jnp.where(held == h, value, 0.0)
                        if not first:
                            term = hyper_acc[c, q, h, other] + term
                        hyper_acc[c, q, h, other] = term

        add_from(here, True)

        def arrive(t):
            fwd_arrival(c, behind(t)).wait_recv()
            add_from(behind(t), False)

        repeat(1, half, arrive)
        mir_send[applied * chunks + c] = hyper_acc[c].astype(BF16)
        mir_copy(applied * chunks + c).start()
        repeat(1, half, lambda t: fwd_copy(c, t).wait_send())

    def answer_all(c, applied):
        mir_copy(applied * chunks + c).wait_recv()
        if c == 0 and not applied:
            scale_copy.wait_recv()
        for q in range(2):
            own = q == v // half
            for other in range(ne):
                scale = jnp.where(own, scale_e[other], scale_m[other])
                for h in range(hyper_blocks):
                    total = hyper_acc[c, q, h, other] + mir_recv[
                        applied * chunks + c, q, h, other
                    ].astype(F32)
                    hyper_feat[q, h, other] = (total * scale[h : h + 1, :]).astype(BF16)

        def answer(t):
            if applied:
                bwd_copy(c, t).wait_send()
            for other in range(ne):
                for q in range(2):
                    held = owner_blocks[(here + t) % half, other, q * half + here]
                    bwd_send[c, t, other, q] = hyper_feat[q, held, other]
            bwd_copy(c, t).start()

        repeat(1, half, answer)
        for other in range(ne):
            for q in range(2):
                held = owner_blocks[here, other, q * half + here]
                bwd_recv[c, here, other, q] = hyper_feat[q, held, other]

    def gather_rows(c):
        def spread(t):
            for q in range(2):
                for j in range(ne):
                    i = t * 2 * ne + q * ne + j
                    value = lax.dot_general(
                        bwd_recv[c, behind(t), edge_at(j), q],
                        tiles[edge_at(j), q * half + behind(t)],
                        (((1,), (1,)), ((), ())),
                        preferred_element_type=F32,
                    )
                    acc[c, i] = value + acc[c, prev[i]]

        spread(0)

        def come_back(t):
            bwd_arrival(c, behind(t)).wait_recv()
            spread(t)

        repeat(1, half, come_back)

    def fin_copy(c, j):
        return to_edge(
            fin_send.at[c, j],
            fin_recv.at[c, e],
            fin_send_sem.at[c, j],
            fin_recv_sem.at[c, e],
            edge_at(j),
        )

    def finish(c):
        for j in range(ne - 1, -1, -1):
            for k in range(share):
                b = edge_at(j) * share + k
                value = (rs[pl.ds(b, 1), :] * acc[c, last[b]]).astype(BF16)
                if j:
                    fin_send[c, j, k] = value
                else:
                    fin_recv[c, e, k] = value
            if j:
                fin_copy(c, j).start()

    for applied in range(2):
        for c in range(chunks):
            sum_half(c, applied)
        for c in range(chunks):
            answer_all(c, applied)
        for c in range(chunks):
            gather_rows(c)
            if applied:
                finish(c)
            else:
                for b in range(blocks):
                    scale = rs[b : b + 1, :]
                    xs[c, b] = (scale * (scale * acc[c, last[b]])).astype(BF16)
                send_again(c)

    for c in range(chunks):
        for j in range(1, ne):
            source = edge_at(j)
            to_edge(
                fin_send.at[c, 0],
                fin_recv.at[c, source],
                fin_send_sem.at[c, 0],
                fin_recv_sem.at[c, source],
                e,
            ).wait_recv()
    for k in range(share):
        for g in range(ne // group):
            stacked = jnp.concatenate(
                [
                    fin_recv[c, g * group + i, k].astype(F32)
                    for i in range(group)
                    for c in range(chunks)
                ],
                axis=0,
            )
            out[pl.ds(k * block, block), pl.ds(g * LANES, LANES)] = stacked.T.astype(BF16)

    for copy in meta_copies + tile_copies + relays:
        copy.wait_send()
    repeat(1, half, lambda t: mv_copy(t).wait_send())
    scale_copy.wait_send()
    for c in range(chunks):
        for applied in range(2):
            mir_copy(applied * chunks + c).wait_send()
        repeat(1, half, lambda t: bwd_copy(c, t).wait_send())
        for j in range(1, ne):
            fin_copy(c, j).wait_send()


def shards(
    features, incidence, send_count, row_block, edge_block, edge_weight, edge_degree, vertex_degree
):
    nv = lax.axis_size("vert")
    ne = lax.axis_size("edge")
    papers, width = features.shape
    slots, block, _ = incidence.shape
    blocks = papers // block
    hyper_blocks = edge_weight.shape[0]
    cols = width // ne
    share = blocks // ne
    half = nv // 2
    chunks = max(1, cols // 32)
    cut = cols // chunks
    scratch = [
        ((papers, LANES), F32),
        ((hyper_blocks, block), F32),
        ((hyper_blocks, block), jnp.int32),
        ((blocks, block), jnp.int32),
        ((ne, slots, block, block), BF16),
        ((ne, 8, LANES), jnp.int32),
        ((ne, 8, LANES), F32),
        ((ne, 8, LANES), F32),
        ((half, 8, LANES), jnp.int32),
        None,
        None,
        ((chunks, blocks, cut, block), BF16),
        ((blocks, block), F32),
        ((chunks, half, ne, 2, cut, block), BF16),
        ((chunks, half, ne, 2, cut, block), BF16),
        ((chunks, half, ne, 2, cut, block), BF16),
        ((chunks, half, ne, 2, cut, block), BF16),
        ((chunks, nv * ne + 1, cut, block), F32),
        None,
        None,
        ((chunks, 2, hyper_blocks, ne, cut, block), F32),
        ((2, hyper_blocks, ne, cut, block), BF16),
        ((2 * chunks, 2, hyper_blocks, ne, cut, block), BF16),
        ((2 * chunks, 2, hyper_blocks, ne, cut, block), BF16),
        ((chunks, ne, share, cut, block), BF16),
        ((chunks, ne, share, cut, block), BF16),
    ]
    scalars = iter(
        [(ne, 8, LANES), (half, 8, LANES), (nv * ne,), (blocks,)]
    )
    held = sum(
        math.prod(item[0]) * jnp.dtype(item[1]).itemsize for item in scratch if item is not None
    )
    held += papers // ne * width * 2
    shapes = [
        pltpu.SMEM(next(scalars), jnp.int32) if item is None else pltpu.VMEM(*item)
        for item in scratch
    ]
    dma = pltpu.SemaphoreType.DMA
    sems = [dma((ne,))] * 7 + [dma((half,))] * 2 + [dma((chunks, half))] * 4
    sems += [dma((chunks, ne))] * 2 + [dma((2 * chunks + 1,))] * 2 + [dma((7,))]
    hbm = pl.BlockSpec(memory_space=pltpu.HBM)
    vmem = pl.BlockSpec(memory_space=pltpu.VMEM)
    smem = pl.BlockSpec(memory_space=pltpu.SMEM)
    return pl.pallas_call(
        functools.partial(kernel, nv, ne, chunks),
        out_shape=jax.ShapeDtypeStruct((papers // ne, width), BF16),
        in_specs=[hbm, hbm, smem, smem, smem, hbm, hbm, hbm],
        out_specs=vmem,
        scratch_shapes=shapes + sems,
        compiler_params=pltpu.CompilerParams(
            collective_id=0,
            has_side_effects=True,
            vmem_limit_bytes=max(held + 6 * 2**20, 60 * 2**20),
        ),
        cost_estimate=pl.CostEstimate(
            flops=8 * slots * ne * block * block * cols,
            bytes_accessed=features.size * 4 + incidence.size * 2,
            transcendentals=0,
        ),
    )(
        features,
        incidence,
        send_count.reshape(1, slots),
        row_block.reshape(1, slots),
        edge_block.reshape(1, slots),
        edge_weight,
        edge_degree,
        vertex_degree.reshape(blocks, block),
    ).astype(F32)


def solution(mesh):
    placed = (
        P("vert", None),
        P("vert", None, "edge"),
        P("vert", "edge"),
        P("vert", "edge"),
        P("vert", "edge"),
        P("vert", "edge"),
        P("vert", "edge"),
        P("vert"),
    )
    return jax.shard_map(
        shards, mesh=mesh, in_specs=placed, out_specs=P(("vert", "edge"), None), check_vma=False
    )
```

```python
import functools
import math

import jax
import jax.numpy as jnp
from jax import lax
from jax.experimental import pallas as pl
from jax.experimental.pallas import tpu as pltpu
from jax.sharding import PartitionSpec as P

MESH = pl.DeviceIdType.MESH
LANES = 128
BF16 = jnp.bfloat16
F32 = jnp.float32


def repeat(start, stop, body):
    @pl.loop(start, stop)
    def _(step):
        body(step)


def kernel(
    nv,
    ne,
    chunks,
    feat,
    inc,
    live_s,
    row_s,
    edge_s,
    weight,
    degree,
    vdeg,
    out,
    mine,
    weight_v,
    degree_v,
    vdeg_v,
    tiles,
    meta_e,
    scale_e,
    scale_m,
    meta_v,
    keys,
    owner_blocks,
    xs,
    rs,
    fwd_send,
    fwd_recv,
    bwd_send,
    bwd_recv,
    acc,
    prev,
    last,
    hyper_acc,
    hyper_feat,
    mir_send,
    mir_recv,
    fin_send,
    fin_recv,
    meta_send_sem,
    meta_recv_sem,
    scale_send_sem,
    scale_recv_sem,
    tile_send_sem,
    tile_recv_sem,
    relay_sem,
    mv_send_sem,
    mv_recv_sem,
    fwd_send_sem,
    fwd_recv_sem,
    bwd_send_sem,
    bwd_recv_sem,
    fin_send_sem,
    fin_recv_sem,
    mir_send_sem,
    mir_recv_sem,
    local_sem,
):
    v = lax.axis_index("vert")
    e = lax.axis_index("edge")
    block = inc.shape[1]
    blocks = xs.shape[1]
    part_cols = xs.shape[2]
    cols = chunks * part_cols
    hyper_blocks = weight.shape[0]
    share = blocks // ne
    none = nv * ne
    half = nv // 2
    here = v % half
    base = v - here
    mirror = (v + half) % nv
    sibling = e + 1 - 2 * (e % 2)

    def edge_at(j):
        first = e + (j % 2) * (sibling - e)
        return (first + 2 * (j // 2)) % ne

    def pair_at(m):
        return pl.ds((e - e % 2 + 2 * m) % ne, 2)

    def ahead(t):
        return base + (here + t) % half

    def behind(t):
        return (here - t + half) % half

    def to_edge(src, dst, send_sem, recv_sem, target):
        return pltpu.make_async_remote_copy(
            src_ref=src,
            dst_ref=dst,
            send_sem=send_sem,
            recv_sem=recv_sem,
            device_id=(v, target),
            device_id_type=MESH,
        )

    def to_vert(src, dst, send_sem, recv_sem, target):
        return pltpu.make_async_remote_copy(
            src_ref=src,
            dst_ref=dst,
            send_sem=send_sem,
            recv_sem=recv_sem,
            device_id=(target, e),
            device_id_type=MESH,
        )

    group = LANES // cols
    start = pl.multiple_of((e // group) * LANES, LANES)
    part = e % group
    fetches = [
        pltpu.make_async_copy(weight, weight_v, local_sem.at[2]),
        pltpu.make_async_copy(degree, degree_v, local_sem.at[3]),
        pltpu.make_async_copy(vdeg, vdeg_v, local_sem.at[4]),
        pltpu.make_async_copy(feat.at[:, pl.ds(start, LANES)], mine, local_sem.at[5]),
        pltpu.make_async_copy(inc, tiles.at[e], local_sem.at[6]),
    ]
    for copy in fetches:
        copy.start()

    barrier = pltpu.get_barrier_semaphore()

    def greet_vert(t):
        pl.semaphore_signal(barrier, inc=1, device_id=(ahead(t), e), device_id_type=MESH)

    repeat(1, half, greet_vert)
    pl.semaphore_signal(barrier, inc=1, device_id=(mirror, e), device_id_type=MESH)
    for j in range(1, ne):
        pl.semaphore_signal(barrier, inc=1, device_id=(v, edge_at(j)), device_id_type=MESH)

    lane = lax.broadcasted_iota(jnp.int32, (8, LANES), 1)
    sub = lax.broadcasted_iota(jnp.int32, (8, LANES), 0)
    packed = jnp.zeros((8, LANES), jnp.int32)
    for s in range(nv):
        key = jnp.where(live_s[0, s] > 0, row_s[0, s], -1)
        both = jnp.where(sub == 0, key, edge_s[0, s])
        packed = jnp.where(lane == s, both, packed)
    meta_e[e] = packed
    for copy in fetches[:2]:
        copy.wait()
    scale_e[e, :hyper_blocks] = weight_v[...] / jnp.maximum(degree_v[...], 1).astype(F32)

    pl.semaphore_wait(barrier, half + ne - 1)

    meta_copies, tile_copies = [], []
    for j in range(1, ne):
        target = edge_at(j)
        meta_copies.append(
            to_edge(
                meta_e.at[e], meta_e.at[e], meta_send_sem.at[j], meta_recv_sem.at[e], target
            )
        )
        meta_copies.append(
            to_edge(
                scale_e.at[e], scale_e.at[e], scale_send_sem.at[j], scale_recv_sem.at[e], target
            )
        )
    for copy in meta_copies:
        copy.start()
    for j in [1] + list(range(2, ne, 2)):
        for q in range(2):
            some = pl.ds(q * half, half)
            copy = to_edge(
                inc.at[some],
                tiles.at[e, some],
                tile_send_sem.at[q, j],
                tile_recv_sem.at[q, e],
                edge_at(j),
            )
            copy.start()
            tile_copies.append(copy)

    for copy in fetches[2:4]:
        copy.wait()
    rs[...] = 1.0 / jnp.sqrt(jnp.maximum(vdeg_v[...], 1).astype(F32))
    unit = math.gcd(blocks, 4)

    def prepare(u):
        for i in range(unit):
            b = u * unit + i
            turned = mine[pl.ds(pl.multiple_of(b * block, block), block), :].T
            picked = turned[:cols]
            for g in range(1, group):
                picked = jnp.where(part == g, turned[g * cols : (g + 1) * cols], picked)
            picked = (picked * rs[pl.ds(b, 1), :]).astype(BF16)
            for c in range(chunks):
                xs[c, b] = picked[c * part_cols : (c + 1) * part_cols]

    repeat(0, blocks // unit, prepare)
    fetches[4].wait()

    def slot_of(j, s):
        if j == 0:
            return live_s[0, s] > 0, row_s[0, s]
        key = keys[edge_at(j), 0, s]
        return key >= 0, jnp.maximum(key, 0)

    def partial(j, s, some):
        alive, row = slot_of(j, s)
        held = [xs[c, row] for c in some]
        left = held[0] if len(held) == 1 else jnp.concatenate(held, axis=0)
        value = jnp.dot(left, tiles[edge_at(j), s], preferred_element_type=F32)
        return jnp.where(alive, value, 0.0).astype(BF16)

    def fwd_copy(c, t):
        return to_vert(
            fwd_send.at[c, t],
            fwd_recv.at[c, here],
            fwd_send_sem.at[c, t],
            fwd_recv_sem.at[c, here],
            ahead(t),
        )

    def fwd_arrival(c, source):
        return to_vert(
            fwd_send.at[c, 0],
            fwd_recv.at[c, source],
            fwd_send_sem.at[c, 0],
            fwd_recv_sem.at[c, source],
            v,
        )

    def bwd_copy(c, t):
        return to_vert(
            bwd_send.at[c, t],
            bwd_recv.at[c, here],
            bwd_send_sem.at[c, t],
            bwd_recv_sem.at[c, here],
            ahead(t),
        )

    def bwd_arrival(c, source):
        return to_vert(
            bwd_send.at[c, 0],
            bwd_recv.at[c, source],
            bwd_send_sem.at[c, 0],
            bwd_recv_sem.at[c, source],
            v,
        )

    def mv_copy(t):
        return to_vert(
            meta_v.at[here], meta_v.at[here], mv_send_sem.at[t], mv_recv_sem.at[here], ahead(t)
        )

    def mv_arrival(source):
        return to_vert(
            meta_v.at[here], meta_v.at[source], mv_send_sem.at[0], mv_recv_sem.at[source], v
        )

    def tile_arrival(q, source):
        some = pl.ds(q * half, half)
        return to_edge(
            inc.at[some],
            tiles.at[source, some],
            tile_send_sem.at[q, 0],
            tile_recv_sem.at[q, source],
            e,
        )

    def mir_copy(p):
        return to_vert(
            mir_send.at[p], mir_recv.at[p], mir_send_sem.at[p], mir_recv_sem.at[p], mirror
        )

    scale_copy = to_vert(
        scale_e, scale_m, mir_send_sem.at[2 * chunks], mir_recv_sem.at[2 * chunks], mirror
    )

    def first_part(j, q):
        other = edge_at(j)

        def step(t):
            value = partial(j, q * half + (here + t) % half, range(chunks))
            for c in range(chunks):
                fwd_send[c, t, other, q] = value[c * part_cols : (c + 1) * part_cols]

        repeat(1, half, step)
        value = partial(j, q * half + here, range(chunks))
        for c in range(chunks):
            fwd_recv[c, here, other, q] = value[c * part_cols : (c + 1) * part_cols]

    def first_pair(m):
        pair = pair_at(m)

        for c in range(chunks):

            def step(t):
                to_vert(
                    fwd_send.at[c, t, pair],
                    fwd_recv.at[c, here, pair],
                    fwd_send_sem.at[c, t],
                    fwd_recv_sem.at[c, here],
                    ahead(t),
                ).start()

            repeat(1, half, step)

    for q in range(2):
        first_part(0, q)

    for j in range(1, ne):
        source = edge_at(j)
        to_edge(
            meta_e.at[e], meta_e.at[source], meta_send_sem.at[0], meta_recv_sem.at[source], e
        ).wait_recv()
        to_edge(
            scale_e.at[e], scale_e.at[source], scale_send_sem.at[0], scale_recv_sem.at[source], e
        ).wait_recv()
    to_scalars = pltpu.make_async_copy(meta_e, keys, local_sem.at[0])
    to_scalars.start()
    seen = jnp.zeros((8, LANES), jnp.int32)
    for other in range(ne):
        seen = jnp.where(sub == other, meta_e[other, 1:2, :], seen)
    meta_v[here] = seen
    repeat(1, half, lambda t: mv_copy(t).start())
    scale_copy.start()
    to_scalars.wait()

    relays = []
    def relay(j, q):
        source = edge_at(j)
        some = pl.ds(q * half, half)
        tile_arrival(q, source).wait_recv()
        if j >= 2 and j % 2 == 0:
            copy = to_edge(
                tiles.at[source, some],
                tiles.at[source, some],
                relay_sem.at[q, j],
                tile_recv_sem.at[q, source],
                sibling,
            )
            copy.start()
            relays.append(copy)

    for q in range(2):
        relay(1, q)
        first_part(1, q)
    first_pair(0)
    for m in range(1, ne // 2):
        for q in range(2):
            relay(2 * m, q)
            first_part(2 * m, q)
        for q in range(2):
            relay(2 * m + 1, q)
            first_part(2 * m + 1, q)
        first_pair(m)

    def link(i, latest):
        slot = ((i // ne) % 2) * half + behind(i // (2 * ne))
        key = keys[edge_at(i % ne), 0, slot]
        before = none
        for b in range(blocks):
            before = jnp.where(key == b, latest[b], before)
        prev[i] = before
        return tuple(jnp.where(key == b, i, latest[b]) for b in range(blocks))

    latest = lax.fori_loop(0, none, link, (jnp.int32(none),) * blocks)
    for b in range(blocks):
        last[b] = latest[b]
    for c in range(chunks):
        acc[c, none] = jnp.zeros(acc.shape[2:], F32)

    repeat(1, half, lambda t: mv_arrival(behind(t)).wait_recv())
    to_scalars = pltpu.make_async_copy(meta_v, owner_blocks, local_sem.at[1])
    to_scalars.start()
    to_scalars.wait()

    def send_again(c):
        def send_all(t):
            for j in range(ne):
                for q in range(2):
                    slot = q * half + (here + t) % half
                    fwd_send[c, t, edge_at(j), q] = partial(j, slot, (c,))
            fwd_copy(c, t).start()

        repeat(1, half, send_all)
        for j in range(ne):
            for q in range(2):
                fwd_recv[c, here, edge_at(j), q] = partial(j, q * half + here, (c,))

    def sum_half(c, applied):
        def add_from(source, first):
            for other in range(ne):
                for q in range(2):
                    held = owner_blocks[source, other, q * half + here]
                    value = fwd_recv[c, source, other, q].astype(F32)
                    for h in range(hyper_blocks):
                        term = jnp.where(held == h, value, 0.0)
                        if not first:
                            term = hyper_acc[c, q, h, other] + term
                        hyper_acc[c, q, h, other] = term

        add_from(here, True)

        def arrive(t):
            fwd_arrival(c, behind(t)).wait_recv()
            add_from(behind(t), False)

        repeat(1, half, arrive)
        mir_send[applied * chunks + c] = hyper_acc[c].astype(BF16)
        mir_copy(applied * chunks + c).start()
        repeat(1, half, lambda t: fwd_copy(c, t).wait_send())

    def answer_all(c, applied):
        mir_copy(applied * chunks + c).wait_recv()
        for q in range(2):
            own = q == v // half
            for other in range(ne):
                scale = jnp.where(own, scale_e[other], scale_m[other])
                for h in range(hyper_blocks):
                    total = hyper_acc[c, q, h, other] + mir_recv[
                        applied * chunks + c, q, h, other
                    ].astype(F32)
                    hyper_feat[q, h, other] = (total * scale[h : h + 1, :]).astype(BF16)

        def answer(t):
            @pl.when(applied > 0)
            def _():
                bwd_copy(c, t).wait_send()

            for other in range(ne):
                for q in range(2):
                    held = owner_blocks[(here + t) % half, other, q * half + here]
                    bwd_send[c, t, other, q] = hyper_feat[q, held, other]
            bwd_copy(c, t).start()

        repeat(1, half, answer)
        for other in range(ne):
            for q in range(2):
                held = owner_blocks[here, other, q * half + here]
                bwd_recv[c, here, other, q] = hyper_feat[q, held, other]

    def gather_rows(c):
        def spread(t):
            for q in range(2):
                for j in range(ne):
                    i = t * 2 * ne + q * ne + j
                    value = lax.dot_general(
                        bwd_recv[c, behind(t), edge_at(j), q],
                        tiles[edge_at(j), q * half + behind(t)],
                        (((1,), (1,)), ((), ())),
                        preferred_element_type=F32,
                    )
                    acc[c, i] = value + acc[c, prev[i]]

        spread(0)

        def come_back(t):
            bwd_arrival(c, behind(t)).wait_recv()
            spread(t)

        repeat(1, half, come_back)

    def fin_copy(c, j):
        return to_edge(
            fin_send.at[c, j],
            fin_recv.at[c, e],
            fin_send_sem.at[c, j],
            fin_recv_sem.at[c, e],
            edge_at(j),
        )

    def finish(c):
        for j in range(ne - 1, -1, -1):
            for k in range(share):
                b = edge_at(j) * share + k
                value = (rs[pl.ds(b, 1), :] * acc[c, last[b]]).astype(BF16)
                if j:
                    fin_send[c, j, k] = value
                else:
                    fin_recv[c, e, k] = value
            if j:
                fin_copy(c, j).start()

    def scale_again(c):
        def rescale(u):
            for i in range(unit):
                b = u * unit + i
                scale = rs[pl.ds(b, 1), :]
                xs[c, b] = (scale * (scale * acc[c, last[b]])).astype(BF16)

        repeat(0, blocks // unit, rescale)

    scale_copy.wait_recv()

    def one_pass(applied):
        repeat(0, chunks, lambda c: sum_half(c, applied))
        repeat(0, chunks, lambda c: answer_all(c, applied))

        def rows(c):
            gather_rows(c)

            @pl.when(applied == 0)
            def _():
                scale_again(c)
                send_again(c)

            @pl.when(applied > 0)
            def _():
                finish(c)

        repeat(0, chunks, rows)

    repeat(0, 2, one_pass)

    for c in range(chunks):
        for j in range(1, ne):
            source = edge_at(j)
            to_edge(
                fin_send.at[c, 0],
                fin_recv.at[c, source],
                fin_send_sem.at[c, 0],
                fin_recv_sem.at[c, source],
                e,
            ).wait_recv()
    for k in range(share):
        for g in range(ne // group):
            stacked = jnp.concatenate(
                [
                    fin_recv[c, g * group + i, k].astype(F32)
                    for i in range(group)
                    for c in range(chunks)
                ],
                axis=0,
            )
            out[pl.ds(k * block, block), pl.ds(g * LANES, LANES)] = stacked.T.astype(BF16)

    for copy in meta_copies + tile_copies + relays:
        copy.wait_send()
    repeat(1, half, lambda t: mv_copy(t).wait_send())
    scale_copy.wait_send()
    for c in range(chunks):
        for applied in range(2):
            mir_copy(applied * chunks + c).wait_send()
        repeat(1, half, lambda t: bwd_copy(c, t).wait_send())
        for j in range(1, ne):
            fin_copy(c, j).wait_send()


def shards(
    features, incidence, send_count, row_block, edge_block, edge_weight, edge_degree, vertex_degree
):
    nv = lax.axis_size("vert")
    ne = lax.axis_size("edge")
    papers, width = features.shape
    slots, block, _ = incidence.shape
    blocks = papers // block
    hyper_blocks = edge_weight.shape[0]
    cols = width // ne
    share = blocks // ne
    half = nv // 2
    chunks = max(1, cols // 32)
    cut = cols // chunks
    scratch = [
        ((papers, LANES), F32),
        ((hyper_blocks, block), F32),
        ((hyper_blocks, block), jnp.int32),
        ((blocks, block), jnp.int32),
        ((ne, slots, block, block), BF16),
        ((ne, 8, LANES), jnp.int32),
        ((ne, 8, LANES), F32),
        ((ne, 8, LANES), F32),
        ((half, 8, LANES), jnp.int32),
        None,
        None,
        ((chunks, blocks, cut, block), BF16),
        ((blocks, block), F32),
        ((chunks, half, ne, 2, cut, block), BF16),
        ((chunks, half, ne, 2, cut, block), BF16),
        ((chunks, half, ne, 2, cut, block), BF16),
        ((chunks, half, ne, 2, cut, block), BF16),
        ((chunks, nv * ne + 1, cut, block), F32),
        None,
        None,
        ((chunks, 2, hyper_blocks, ne, cut, block), F32),
        ((2, hyper_blocks, ne, cut, block), BF16),
        ((2 * chunks, 2, hyper_blocks, ne, cut, block), BF16),
        ((2 * chunks, 2, hyper_blocks, ne, cut, block), BF16),
        ((chunks, ne, share, cut, block), BF16),
        ((chunks, ne, share, cut, block), BF16),
    ]
    scalars = iter(
        [(ne, 8, LANES), (half, 8, LANES), (nv * ne,), (blocks,)]
    )
    held = sum(
        math.prod(item[0]) * jnp.dtype(item[1]).itemsize for item in scratch if item is not None
    )
    held += papers // ne * width * 2
    shapes = [
        pltpu.SMEM(next(scalars), jnp.int32) if item is None else pltpu.VMEM(*item)
        for item in scratch
    ]
    dma = pltpu.SemaphoreType.DMA
    sems = [dma((ne,))] * 4 + [dma((2, ne))] * 3 + [dma((half,))] * 2 + [dma((chunks, half))] * 4
    sems += [dma((chunks, ne))] * 2 + [dma((2 * chunks + 1,))] * 2 + [dma((7,))]
    hbm = pl.BlockSpec(memory_space=pltpu.HBM)
    vmem = pl.BlockSpec(memory_space=pltpu.VMEM)
    smem = pl.BlockSpec(memory_space=pltpu.SMEM)
    return pl.pallas_call(
        functools.partial(kernel, nv, ne, chunks),
        out_shape=jax.ShapeDtypeStruct((papers // ne, width), BF16),
        in_specs=[hbm, hbm, smem, smem, smem, hbm, hbm, hbm],
        out_specs=vmem,
        scratch_shapes=shapes + sems,
        compiler_params=pltpu.CompilerParams(
            collective_id=0,
            has_side_effects=True,
            vmem_limit_bytes=max(held + 6 * 2**20, 60 * 2**20),
        ),
        cost_estimate=pl.CostEstimate(
            flops=8 * slots * ne * block * block * cols,
            bytes_accessed=features.size * 4 + incidence.size * 2,
            transcendentals=0,
        ),
    )(
        features,
        incidence,
        send_count.reshape(1, slots),
        row_block.reshape(1, slots),
        edge_block.reshape(1, slots),
        edge_weight,
        edge_degree,
        vertex_degree.reshape(blocks, block),
    ).astype(F32)


def solution(mesh):
    placed = (
        P("vert", None),
        P("vert", None, "edge"),
        P("vert", "edge"),
        P("vert", "edge"),
        P("vert", "edge"),
        P("vert", "edge"),
        P("vert", "edge"),
        P("vert"),
    )
    return jax.shard_map(
        shards, mesh=mesh, in_specs=placed, out_specs=P(("vert", "edge"), None), check_vma=False
    )
```

```python
import functools
import math

import jax
import jax.numpy as jnp
from jax import lax
from jax.experimental import pallas as pl
from jax.experimental.pallas import tpu as pltpu
from jax.sharding import PartitionSpec as P

MESH = pl.DeviceIdType.MESH
LANES = 128
BF16 = jnp.bfloat16
F32 = jnp.float32


def repeat(start, stop, body):
    @pl.loop(start, stop)
    def _(step):
        body(step)


def kernel(
    nv,
    ne,
    feat,
    inc,
    live_s,
    row_s,
    edge_s,
    weight,
    degree,
    vdeg,
    out,
    mine,
    weight_v,
    degree_v,
    vdeg_v,
    tiles,
    meta_e,
    scale_e,
    scale_m,
    meta_v,
    keys,
    owner_blocks,
    xs,
    rs,
    fwd_send,
    fwd_recv,
    bwd_send,
    bwd_recv,
    acc,
    prev,
    last,
    hyper_acc,
    hyper_feat,
    mir_send,
    mir_recv,
    fin_send,
    fin_recv,
    meta_send_sem,
    meta_recv_sem,
    scale_send_sem,
    scale_recv_sem,
    tile_send_sem,
    tile_recv_sem,
    relay_sem,
    mv_send_sem,
    mv_recv_sem,
    fwd_send_sem,
    fwd_recv_sem,
    bwd_send_sem,
    bwd_recv_sem,
    fin_send_sem,
    fin_recv_sem,
    mir_send_sem,
    mir_recv_sem,
    local_sem,
):
    v = lax.axis_index("vert")
    e = lax.axis_index("edge")
    block = inc.shape[1]
    blocks = xs.shape[0]
    cols = xs.shape[1]
    pairs = ne // 2
    hyper_blocks = weight.shape[0]
    share = blocks // ne
    none = nv * ne
    half = nv // 2
    here = v % half
    base = v - here
    mirror = (v + half) % nv
    sibling = e + 1 - 2 * (e % 2)

    def edge_at(j):
        first = e + (j % 2) * (sibling - e)
        return (first + 2 * (j // 2)) % ne

    def edge_of(m, pos):
        return (e - e % 2 + 2 * m) % ne + pos

    def ahead(t):
        return base + (here + t) % half

    def behind(t):
        return (here - t + half) % half

    def to_edge(src, dst, send_sem, recv_sem, target):
        return pltpu.make_async_remote_copy(
            src_ref=src,
            dst_ref=dst,
            send_sem=send_sem,
            recv_sem=recv_sem,
            device_id=(v, target),
            device_id_type=MESH,
        )

    def to_vert(src, dst, send_sem, recv_sem, target):
        return pltpu.make_async_remote_copy(
            src_ref=src,
            dst_ref=dst,
            send_sem=send_sem,
            recv_sem=recv_sem,
            device_id=(target, e),
            device_id_type=MESH,
        )

    group = LANES // cols
    start = pl.multiple_of((e // group) * LANES, LANES)
    part = e % group
    fetches = [
        pltpu.make_async_copy(weight, weight_v, local_sem.at[2]),
        pltpu.make_async_copy(degree, degree_v, local_sem.at[3]),
        pltpu.make_async_copy(vdeg, vdeg_v, local_sem.at[4]),
        pltpu.make_async_copy(feat.at[:, pl.ds(start, LANES)], mine, local_sem.at[5]),
        pltpu.make_async_copy(inc, tiles.at[e], local_sem.at[6]),
    ]
    for copy in fetches:
        copy.start()

    barrier = pltpu.get_barrier_semaphore()

    def greet_vert(t):
        pl.semaphore_signal(barrier, inc=1, device_id=(ahead(t), e), device_id_type=MESH)

    repeat(1, half, greet_vert)
    pl.semaphore_signal(barrier, inc=1, device_id=(mirror, e), device_id_type=MESH)
    for j in range(1, ne):
        pl.semaphore_signal(barrier, inc=1, device_id=(v, edge_at(j)), device_id_type=MESH)

    lane = lax.broadcasted_iota(jnp.int32, (8, LANES), 1)
    sub = lax.broadcasted_iota(jnp.int32, (8, LANES), 0)
    packed = jnp.zeros((8, LANES), jnp.int32)
    for s in range(nv):
        key = jnp.where(live_s[0, s] > 0, row_s[0, s], -1)
        both = jnp.where(sub == 0, key, edge_s[0, s])
        packed = jnp.where(lane == s, both, packed)
    meta_e[e] = packed
    for copy in fetches[:2]:
        copy.wait()
    scale_e[e, :hyper_blocks] = weight_v[...] / jnp.maximum(degree_v[...], 1).astype(F32)

    pl.semaphore_wait(barrier, half + ne - 1)

    meta_copies, tile_copies = [], []
    for j in range(1, ne):
        target = edge_at(j)
        meta_copies.append(
            to_edge(
                meta_e.at[e], meta_e.at[e], meta_send_sem.at[j], meta_recv_sem.at[e], target
            )
        )
        meta_copies.append(
            to_edge(
                scale_e.at[e], scale_e.at[e], scale_send_sem.at[j], scale_recv_sem.at[e], target
            )
        )
    for copy in meta_copies:
        copy.start()
    for j in [1] + list(range(2, ne, 2)):
        for q in range(2):
            some = pl.ds(q * half, half)
            copy = to_edge(
                inc.at[some],
                tiles.at[e, some],
                tile_send_sem.at[q, j],
                tile_recv_sem.at[q, e],
                edge_at(j),
            )
            copy.start()
            tile_copies.append(copy)

    for copy in fetches[2:4]:
        copy.wait()
    rs[...] = 1.0 / jnp.sqrt(jnp.maximum(vdeg_v[...], 1).astype(F32))
    unit = math.gcd(blocks, 4)

    def prepare(u):
        for i in range(unit):
            b = u * unit + i
            turned = mine[pl.ds(pl.multiple_of(b * block, block), block), :].T
            picked = turned[:cols]
            for g in range(1, group):
                picked = jnp.where(part == g, turned[g * cols : (g + 1) * cols], picked)
            picked = (picked * rs[pl.ds(b, 1), :]).astype(BF16)
            xs[b] = picked

    repeat(0, blocks // unit, prepare)
    fetches[4].wait()

    def partial(other, s):
        key = keys[other, 0, s]
        value = jnp.dot(
            xs[jnp.maximum(key, 0)], tiles[other, s], preferred_element_type=F32
        )
        return jnp.where(key >= 0, value, 0.0).astype(BF16)

    def fwd_copy(c, t):
        return to_vert(
            fwd_send.at[c, t],
            fwd_recv.at[c, here],
            fwd_send_sem.at[c, t],
            fwd_recv_sem.at[c, here],
            ahead(t),
        )

    def fwd_arrival(c, source):
        return to_vert(
            fwd_send.at[c, 0],
            fwd_recv.at[c, source],
            fwd_send_sem.at[c, 0],
            fwd_recv_sem.at[c, source],
            v,
        )

    def bwd_copy(c, t):
        return to_vert(
            bwd_send.at[c, t],
            bwd_recv.at[c, here],
            bwd_send_sem.at[c, t],
            bwd_recv_sem.at[c, here],
            ahead(t),
        )

    def bwd_arrival(c, source):
        return to_vert(
            bwd_send.at[c, 0],
            bwd_recv.at[c, source],
            bwd_send_sem.at[c, 0],
            bwd_recv_sem.at[c, source],
            v,
        )

    def mv_copy(t):
        return to_vert(
            meta_v.at[here], meta_v.at[here], mv_send_sem.at[t], mv_recv_sem.at[here], ahead(t)
        )

    def mv_arrival(source):
        return to_vert(
            meta_v.at[here], meta_v.at[source], mv_send_sem.at[0], mv_recv_sem.at[source], v
        )

    def tile_arrival(q, source):
        some = pl.ds(q * half, half)
        return to_edge(
            inc.at[some],
            tiles.at[source, some],
            tile_send_sem.at[q, 0],
            tile_recv_sem.at[q, source],
            e,
        )

    def mir_copy(p):
        return to_vert(
            mir_send.at[p], mir_recv.at[p], mir_send_sem.at[p], mir_recv_sem.at[p], mirror
        )

    scale_copy = to_vert(
        scale_e, scale_m, mir_send_sem.at[2 * pairs], mir_recv_sem.at[2 * pairs], mirror
    )

    for j in range(1, ne):
        source = edge_at(j)
        to_edge(
            meta_e.at[e], meta_e.at[source], meta_send_sem.at[0], meta_recv_sem.at[source], e
        ).wait_recv()
        to_edge(
            scale_e.at[e], scale_e.at[source], scale_send_sem.at[0], scale_recv_sem.at[source], e
        ).wait_recv()
    to_scalars = pltpu.make_async_copy(meta_e, keys, local_sem.at[0])
    to_scalars.start()
    seen = jnp.zeros((8, LANES), jnp.int32)
    for other in range(ne):
        seen = jnp.where(sub == other, meta_e[other, 1:2, :], seen)
    meta_v[here] = seen
    repeat(1, half, lambda t: mv_copy(t).start())
    scale_copy.start()
    to_scalars.wait()

    relays = []
    def relay(j, q):
        source = edge_at(j)
        some = pl.ds(q * half, half)
        tile_arrival(q, source).wait_recv()
        if j >= 2 and j % 2 == 0:
            copy = to_edge(
                tiles.at[source, some],
                tiles.at[source, some],
                relay_sem.at[q, j],
                tile_recv_sem.at[q, source],
                sibling,
            )
            copy.start()
            relays.append(copy)

    def send_all(m):
        def step(t):
            for pos in range(2):
                for q in range(2):
                    slot = q * half + (here + t) % half
                    fwd_send[m, t, pos, q] = partial(edge_of(m, pos), slot)
            fwd_copy(m, t).start()

        repeat(1, half, step)
        for pos in range(2):
            for q in range(2):
                fwd_recv[m, here, pos, q] = partial(edge_of(m, pos), q * half + here)

    def sum_half(m, applied):
        def add_from(source, first):
            for pos in range(2):
                for q in range(2):
                    held = owner_blocks[source, edge_of(m, pos), q * half + here]
                    value = fwd_recv[m, source, pos, q].astype(F32)
                    for h in range(hyper_blocks):
                        term = jnp.where(held == h, value, 0.0)
                        if not first:
                            term = hyper_acc[m, q, h, pos] + term
                        hyper_acc[m, q, h, pos] = term

        add_from(here, True)

        def arrive(t):
            fwd_arrival(m, behind(t)).wait_recv()
            add_from(behind(t), False)

        repeat(1, half, arrive)
        mir_send[applied * pairs + m] = hyper_acc[m].astype(BF16)
        mir_copy(applied * pairs + m).start()
        repeat(1, half, lambda t: fwd_copy(m, t).wait_send())

    def answer_all(m, applied):
        p = applied * pairs + m
        mir_copy(p).wait_recv()
        for q in range(2):
            own = q == v // half
            for pos in range(2):
                other = edge_of(m, pos)
                scale = jnp.where(own, scale_e[other], scale_m[other])
                for h in range(hyper_blocks):
                    total = hyper_acc[m, q, h, pos] + mir_recv[p, q, h, pos].astype(F32)
                    hyper_feat[q, h, pos] = (total * scale[h : h + 1, :]).astype(BF16)

        def answer(t):
            if applied:
                bwd_copy(m, t).wait_send()
            for pos in range(2):
                for q in range(2):
                    held = owner_blocks[(here + t) % half, edge_of(m, pos), q * half + here]
                    bwd_send[m, t, pos, q] = hyper_feat[q, held, pos]
            bwd_copy(m, t).start()

        repeat(1, half, answer)
        for pos in range(2):
            for q in range(2):
                held = owner_blocks[here, edge_of(m, pos), q * half + here]
                bwd_recv[m, here, pos, q] = hyper_feat[q, held, pos]

    def gather_rows(m):
        def spread(t):
            values = [
                lax.dot_general(
                    bwd_recv[m, behind(t), pos, q],
                    tiles[edge_of(m, pos), q * half + behind(t)],
                    (((1,), (1,)), ((), ())),
                    preferred_element_type=F32,
                )
                for q in range(2)
                for pos in range(2)
            ]
            for n, value in enumerate(values):
                i = (m * half + t) * 4 + n
                acc[i] = value + acc[prev[i]]

        spread(0)

        def come_back(t):
            bwd_arrival(m, behind(t)).wait_recv()
            spread(t)

        repeat(1, half, come_back)

    def scale_again(u):
        for i in range(unit):
            b = u * unit + i
            scale = rs[pl.ds(b, 1), :]
            xs[b] = (scale * (scale * acc[last[b]])).astype(BF16)

    for q in range(2):
        relay(1, q)
    send_all(0)
    def link(i, latest):
        other = edge_of(i // (4 * half), i % 2)
        slot = ((i // 2) % 2) * half + behind((i // 4) % half)
        key = keys[other, 0, slot]
        before = none
        for b in range(blocks):
            before = jnp.where(key == b, latest[b], before)
        prev[i] = before
        return tuple(jnp.where(key == b, i, latest[b]) for b in range(blocks))

    latest = lax.fori_loop(0, none, link, (jnp.int32(none),) * blocks)
    for b in range(blocks):
        last[b] = latest[b]
    acc[none] = jnp.zeros(acc.shape[1:], F32)

    repeat(1, half, lambda t: mv_arrival(behind(t)).wait_recv())
    to_scalars = pltpu.make_async_copy(meta_v, owner_blocks, local_sem.at[1])
    to_scalars.start()
    to_scalars.wait()

    for m in range(1, pairs):
        for q in range(2):
            relay(2 * m, q)
    sum_half(0, 0)
    for m in range(1, pairs):
        for q in range(2):
            relay(2 * m + 1, q)
        send_all(m)
        sum_half(m, 0)
    scale_copy.wait_recv()

    for applied in range(2):
        if applied:
            for m in range(pairs):
                send_all(m)
            for m in range(pairs):
                sum_half(m, 1)
        for m in range(pairs):
            answer_all(m, applied)
        for m in range(pairs):
            gather_rows(m)
        if not applied:
            repeat(0, blocks // unit, scale_again)

    def fin_copy(j):
        return to_edge(
            fin_send.at[j], fin_recv.at[e], fin_send_sem.at[j], fin_recv_sem.at[e], edge_at(j)
        )

    for j in range(ne - 1, -1, -1):
        for k in range(share):
            b = edge_at(j) * share + k
            value = (rs[pl.ds(b, 1), :] * acc[last[b]]).astype(BF16)
            if j:
                fin_send[j, k] = value
            else:
                fin_recv[e, k] = value
        if j:
            fin_copy(j).start()
    for j in range(1, ne):
        source = edge_at(j)
        to_edge(
            fin_send.at[0], fin_recv.at[source], fin_send_sem.at[0], fin_recv_sem.at[source], e
        ).wait_recv()
    for k in range(share):
        for g in range(ne // group):
            stacked = jnp.concatenate(
                [
                    fin_recv[g * group + i, k].astype(F32)
                    for i in range(group)
                ],
                axis=0,
            )
            out[pl.ds(k * block, block), pl.ds(g * LANES, LANES)] = stacked.T.astype(BF16)

    for copy in meta_copies + tile_copies + relays:
        copy.wait_send()
    repeat(1, half, lambda t: mv_copy(t).wait_send())
    scale_copy.wait_send()
    for m in range(pairs):
        for applied in range(2):
            mir_copy(applied * pairs + m).wait_send()
        repeat(1, half, lambda t: bwd_copy(m, t).wait_send())
    for j in range(1, ne):
        fin_copy(j).wait_send()


def shards(
    features, incidence, send_count, row_block, edge_block, edge_weight, edge_degree, vertex_degree
):
    nv = lax.axis_size("vert")
    ne = lax.axis_size("edge")
    papers, width = features.shape
    slots, block, _ = incidence.shape
    blocks = papers // block
    hyper_blocks = edge_weight.shape[0]
    cols = width // ne
    share = blocks // ne
    half = nv // 2
    pairs = ne // 2
    scratch = [
        ((papers, LANES), F32),
        ((hyper_blocks, block), F32),
        ((hyper_blocks, block), jnp.int32),
        ((blocks, block), jnp.int32),
        ((ne, slots, block, block), BF16),
        ((ne, 8, LANES), jnp.int32),
        ((ne, 8, LANES), F32),
        ((ne, 8, LANES), F32),
        ((half, 8, LANES), jnp.int32),
        None,
        None,
        ((blocks, cols, block), BF16),
        ((blocks, block), F32),
        ((pairs, half, 2, 2, cols, block), BF16),
        ((pairs, half, 2, 2, cols, block), BF16),
        ((pairs, half, 2, 2, cols, block), BF16),
        ((pairs, half, 2, 2, cols, block), BF16),
        ((nv * ne + 1, cols, block), F32),
        None,
        None,
        ((pairs, 2, hyper_blocks, 2, cols, block), F32),
        ((2, hyper_blocks, 2, cols, block), BF16),
        ((2 * pairs, 2, hyper_blocks, 2, cols, block), BF16),
        ((2 * pairs, 2, hyper_blocks, 2, cols, block), BF16),
        ((ne, share, cols, block), BF16),
        ((ne, share, cols, block), BF16),
    ]
    scalars = iter(
        [(ne, 8, LANES), (half, 8, LANES), (nv * ne,), (blocks,)]
    )
    held = sum(
        math.prod(item[0]) * jnp.dtype(item[1]).itemsize for item in scratch if item is not None
    )
    held += papers // ne * width * 2
    shapes = [
        pltpu.SMEM(next(scalars), jnp.int32) if item is None else pltpu.VMEM(*item)
        for item in scratch
    ]
    dma = pltpu.SemaphoreType.DMA
    sems = [dma((ne,))] * 4 + [dma((2, ne))] * 3 + [dma((half,))] * 2 + [dma((pairs, half))] * 4
    sems += [dma((ne,))] * 2 + [dma((2 * pairs + 1,))] * 2 + [dma((7,))]
    hbm = pl.BlockSpec(memory_space=pltpu.HBM)
    vmem = pl.BlockSpec(memory_space=pltpu.VMEM)
    smem = pl.BlockSpec(memory_space=pltpu.SMEM)
    return pl.pallas_call(
        functools.partial(kernel, nv, ne),
        out_shape=jax.ShapeDtypeStruct((papers // ne, width), BF16),
        in_specs=[hbm, hbm, smem, smem, smem, hbm, hbm, hbm],
        out_specs=vmem,
        scratch_shapes=shapes + sems,
        compiler_params=pltpu.CompilerParams(
            collective_id=0,
            has_side_effects=True,
            vmem_limit_bytes=max(held + 6 * 2**20, 60 * 2**20),
        ),
        cost_estimate=pl.CostEstimate(
            flops=8 * slots * ne * block * block * cols,
            bytes_accessed=features.size * 4 + incidence.size * 2,
            transcendentals=0,
        ),
    )(
        features,
        incidence,
        send_count.reshape(1, slots),
        row_block.reshape(1, slots),
        edge_block.reshape(1, slots),
        edge_weight,
        edge_degree,
        vertex_degree.reshape(blocks, block),
    ).astype(F32)


def solution(mesh):
    placed = (
        P("vert", None),
        P("vert", None, "edge"),
        P("vert", "edge"),
        P("vert", "edge"),
        P("vert", "edge"),
        P("vert", "edge"),
        P("vert", "edge"),
        P("vert"),
    )
    return jax.shard_map(
        shards, mesh=mesh, in_specs=placed, out_specs=P(("vert", "edge"), None), check_vma=False
    )
```

```python
import functools
import math

import jax
import jax.numpy as jnp
from jax import lax
from jax.experimental import pallas as pl
from jax.experimental.pallas import tpu as pltpu
from jax.sharding import PartitionSpec as P

MESH = pl.DeviceIdType.MESH
LANES = 128
BF16 = jnp.bfloat16
F32 = jnp.float32


def repeat(start, stop, body):
    @pl.loop(start, stop)
    def _(step):
        body(step)


def kernel(
    nv,
    ne,
    feat,
    inc,
    live_s,
    row_s,
    edge_s,
    weight,
    degree,
    vdeg,
    out,
    mine,
    weight_v,
    degree_v,
    vdeg_v,
    tiles,
    meta_e,
    scale_e,
    scale_m,
    meta_v,
    keys,
    owner_blocks,
    xs,
    rs,
    fwd_send,
    fwd_recv,
    bwd_send,
    bwd_recv,
    acc,
    prev,
    last,
    hyper_acc,
    hyper_feat,
    mir_send,
    mir_recv,
    fin_send,
    fin_recv,
    meta_send_sem,
    meta_recv_sem,
    scale_send_sem,
    scale_recv_sem,
    tile_send_sem,
    tile_recv_sem,
    relay_sem,
    mv_send_sem,
    mv_recv_sem,
    fwd_send_sem,
    fwd_recv_sem,
    bwd_send_sem,
    bwd_recv_sem,
    fin_send_sem,
    fin_recv_sem,
    mir_send_sem,
    mir_recv_sem,
    local_sem,
):
    v = lax.axis_index("vert")
    e = lax.axis_index("edge")
    block = inc.shape[1]
    blocks = xs.shape[0]
    cols = xs.shape[1]
    hyper_blocks = weight.shape[0]
    share = blocks // ne
    none = nv * ne
    half = nv // 2
    here = v % half
    base = v - here
    mirror = (v + half) % nv
    sibling = e + 1 - 2 * (e % 2)

    def edge_at(j):
        first = e + (j % 2) * (sibling - e)
        return (first + 2 * (j // 2)) % ne

    def ahead(t):
        return base + (here + t) % half

    def behind(t):
        return (here - t + half) % half

    def to_edge(src, dst, send_sem, recv_sem, target):
        return pltpu.make_async_remote_copy(
            src_ref=src,
            dst_ref=dst,
            send_sem=send_sem,
            recv_sem=recv_sem,
            device_id=(v, target),
            device_id_type=MESH,
        )

    def to_vert(src, dst, send_sem, recv_sem, target):
        return pltpu.make_async_remote_copy(
            src_ref=src,
            dst_ref=dst,
            send_sem=send_sem,
            recv_sem=recv_sem,
            device_id=(target, e),
            device_id_type=MESH,
        )

    group = LANES // cols
    start = pl.multiple_of((e // group) * LANES, LANES)
    part = e % group
    fetches = [
        pltpu.make_async_copy(weight, weight_v, local_sem.at[2]),
        pltpu.make_async_copy(degree, degree_v, local_sem.at[3]),
        pltpu.make_async_copy(vdeg, vdeg_v, local_sem.at[4]),
        pltpu.make_async_copy(feat.at[:, pl.ds(start, LANES)], mine, local_sem.at[5]),
        pltpu.make_async_copy(inc, tiles.at[e], local_sem.at[6]),
    ]
    for copy in fetches:
        copy.start()

    barrier = pltpu.get_barrier_semaphore()

    def greet_vert(t):
        pl.semaphore_signal(barrier, inc=1, device_id=(ahead(t), e), device_id_type=MESH)

    repeat(1, half, greet_vert)
    pl.semaphore_signal(barrier, inc=1, device_id=(mirror, e), device_id_type=MESH)
    for j in range(1, ne):
        pl.semaphore_signal(barrier, inc=1, device_id=(v, edge_at(j)), device_id_type=MESH)

    lane = lax.broadcasted_iota(jnp.int32, (8, LANES), 1)
    sub = lax.broadcasted_iota(jnp.int32, (8, LANES), 0)
    packed = jnp.zeros((8, LANES), jnp.int32)
    for s in range(nv):
        key = jnp.where(live_s[0, s] > 0, row_s[0, s], -1)
        both = jnp.where(sub == 0, key, edge_s[0, s])
        packed = jnp.where(lane == s, both, packed)
    meta_e[e] = packed
    for copy in fetches[:2]:
        copy.wait()
    scale_e[e, :hyper_blocks] = weight_v[...] / jnp.maximum(degree_v[...], 1).astype(F32)

    pl.semaphore_wait(barrier, half + ne - 1)

    meta_copies, tile_copies = [], []
    for j in range(1, ne):
        target = edge_at(j)
        meta_copies.append(
            to_edge(
                meta_e.at[e], meta_e.at[e], meta_send_sem.at[j], meta_recv_sem.at[e], target
            )
        )
        meta_copies.append(
            to_edge(
                scale_e.at[e], scale_e.at[e], scale_send_sem.at[j], scale_recv_sem.at[e], target
            )
        )
    for copy in meta_copies:
        copy.start()
    for j in [1] + list(range(2, ne, 2)):
        for q in range(2):
            some = pl.ds(q * half, half)
            copy = to_edge(
                inc.at[some],
                tiles.at[e, some],
                tile_send_sem.at[q, j],
                tile_recv_sem.at[q, e],
                edge_at(j),
            )
            copy.start()
            tile_copies.append(copy)

    for copy in fetches[2:4]:
        copy.wait()
    rs[...] = 1.0 / jnp.sqrt(jnp.maximum(vdeg_v[...], 1).astype(F32))
    unit = math.gcd(blocks, 4)

    def prepare(u):
        for i in range(unit):
            b = u * unit + i
            turned = mine[pl.ds(pl.multiple_of(b * block, block), block), :].T
            picked = turned[:cols]
            for g in range(1, group):
                picked = jnp.where(part == g, turned[g * cols : (g + 1) * cols], picked)
            picked = (picked * rs[pl.ds(b, 1), :]).astype(BF16)
            xs[b] = picked

    repeat(0, blocks // unit, prepare)
    fetches[4].wait()

    def partial(other, s):
        key = keys[other, 0, s]
        value = jnp.dot(
            xs[jnp.maximum(key, 0)], tiles[other, s], preferred_element_type=F32
        )
        return jnp.where(key >= 0, value, 0.0).astype(BF16)

    def fwd_copy(c, t):
        return to_vert(
            fwd_send.at[c, t],
            fwd_recv.at[c, here],
            fwd_send_sem.at[c, t],
            fwd_recv_sem.at[c, here],
            ahead(t),
        )

    def fwd_arrival(c, source):
        return to_vert(
            fwd_send.at[c, 0],
            fwd_recv.at[c, source],
            fwd_send_sem.at[c, 0],
            fwd_recv_sem.at[c, source],
            v,
        )

    def bwd_copy(c, t):
        return to_vert(
            bwd_send.at[c, t],
            bwd_recv.at[c, here],
            bwd_send_sem.at[c, t],
            bwd_recv_sem.at[c, here],
            ahead(t),
        )

    def bwd_arrival(c, source):
        return to_vert(
            bwd_send.at[c, 0],
            bwd_recv.at[c, source],
            bwd_send_sem.at[c, 0],
            bwd_recv_sem.at[c, source],
            v,
        )

    def mv_copy(t):
        return to_vert(
            meta_v.at[here], meta_v.at[here], mv_send_sem.at[t], mv_recv_sem.at[here], ahead(t)
        )

    def mv_arrival(source):
        return to_vert(
            meta_v.at[here], meta_v.at[source], mv_send_sem.at[0], mv_recv_sem.at[source], v
        )

    def tile_arrival(q, source):
        some = pl.ds(q * half, half)
        return to_edge(
            inc.at[some],
            tiles.at[source, some],
            tile_send_sem.at[q, 0],
            tile_recv_sem.at[q, source],
            e,
        )

    def mir_copy(p):
        return to_vert(
            mir_send.at[p], mir_recv.at[p], mir_send_sem.at[p], mir_recv_sem.at[p], mirror
        )

    scale_copy = to_vert(
        scale_e, scale_m, mir_send_sem.at[2 * ne], mir_recv_sem.at[2 * ne], mirror
    )

    for j in range(1, ne):
        source = edge_at(j)
        to_edge(
            meta_e.at[e], meta_e.at[source], meta_send_sem.at[0], meta_recv_sem.at[source], e
        ).wait_recv()
        to_edge(
            scale_e.at[e], scale_e.at[source], scale_send_sem.at[0], scale_recv_sem.at[source], e
        ).wait_recv()
    to_scalars = pltpu.make_async_copy(meta_e, keys, local_sem.at[0])
    to_scalars.start()
    seen = jnp.zeros((8, LANES), jnp.int32)
    for other in range(ne):
        seen = jnp.where(sub == other, meta_e[other, 1:2, :], seen)
    meta_v[here] = seen
    repeat(1, half, lambda t: mv_copy(t).start())
    scale_copy.start()
    to_scalars.wait()

    relays = []
    def relay(j, q):
        source = edge_at(j)
        some = pl.ds(q * half, half)
        tile_arrival(q, source).wait_recv()
        if j >= 2 and j % 2 == 0:
            copy = to_edge(
                tiles.at[source, some],
                tiles.at[source, some],
                relay_sem.at[q, j],
                tile_recv_sem.at[q, source],
                sibling,
            )
            copy.start()
            relays.append(copy)

    def send_all(m, again=False):
        def step(t):
            if again:
                fwd_copy(m, t).wait_send()
            for q in range(2):
                fwd_send[m, t, q] = partial(edge_at(m), q * half + (here + t) % half)
            fwd_copy(m, t).start()

        repeat(1, half, step)
        for q in range(2):
            fwd_recv[m, here, q] = partial(edge_at(m), q * half + here)

    def sum_half(m, applied):
        def add_from(source, first):
            for q in range(2):
                held = owner_blocks[source, edge_at(m), q * half + here]
                value = fwd_recv[m, source, q].astype(F32)
                for h in range(hyper_blocks):
                    term = jnp.where(held == h, value, 0.0)
                    if not first:
                        term = hyper_acc[m, q, h] + term
                    hyper_acc[m, q, h] = term

        add_from(here, True)

        def arrive(t):
            fwd_arrival(m, behind(t)).wait_recv()
            add_from(behind(t), False)

        repeat(1, half, arrive)
        mir_send[applied * ne + m] = hyper_acc[m].astype(BF16)
        mir_copy(applied * ne + m).start()

    def answer_all(m, applied):
        p = applied * ne + m
        mir_copy(p).wait_recv()
        for q in range(2):
            own = q == v // half
            scale = jnp.where(own, scale_e[edge_at(m)], scale_m[edge_at(m)])
            for h in range(hyper_blocks):
                total = hyper_acc[m, q, h] + mir_recv[p, q, h].astype(F32)
                hyper_feat[q, h] = (total * scale[h : h + 1, :]).astype(BF16)

        def answer(t):
            if applied:
                bwd_copy(m, t).wait_send()
            for q in range(2):
                held = owner_blocks[(here + t) % half, edge_at(m), q * half + here]
                bwd_send[m, t, q] = hyper_feat[q, held]
            bwd_copy(m, t).start()

        repeat(1, half, answer)
        for q in range(2):
            held = owner_blocks[here, edge_at(m), q * half + here]
            bwd_recv[m, here, q] = hyper_feat[q, held]

    def gather_rows(m):
        def spread(t):
            values = [
                lax.dot_general(
                    bwd_recv[m, behind(t), q],
                    tiles[edge_at(m), q * half + behind(t)],
                    (((1,), (1,)), ((), ())),
                    preferred_element_type=F32,
                )
                for q in range(2)
            ]
            for n, value in enumerate(values):
                i = (m * half + t) * 2 + n
                acc[i] = value + acc[prev[i]]

        spread(0)

        def come_back(t):
            bwd_arrival(m, behind(t)).wait_recv()
            spread(t)

        repeat(1, half, come_back)

    def scale_again(u):
        for i in range(unit):
            b = u * unit + i
            scale = rs[pl.ds(b, 1), :]
            xs[b] = (scale * (scale * acc[last[b]])).astype(BF16)

    send_all(0)
    for q in range(2):
        relay(1, q)
    send_all(1)
    def link(i, latest):
        other = edge_at(i // (2 * half))
        slot = (i % 2) * half + behind((i // 2) % half)
        key = keys[other, 0, slot]
        before = none
        for b in range(blocks):
            before = jnp.where(key == b, latest[b], before)
        prev[i] = before
        return tuple(jnp.where(key == b, i, latest[b]) for b in range(blocks))

    latest = lax.fori_loop(0, none, link, (jnp.int32(none),) * blocks)
    for b in range(blocks):
        last[b] = latest[b]
    acc[none] = jnp.zeros(acc.shape[1:], F32)

    repeat(1, half, lambda t: mv_arrival(behind(t)).wait_recv())
    to_scalars = pltpu.make_async_copy(meta_v, owner_blocks, local_sem.at[1])
    to_scalars.start()
    to_scalars.wait()

    for m in range(2, ne):
        sum_half(m - 2, 0)
        for q in range(2):
            relay(m, q)
        send_all(m)
    for m in range(ne - 2, ne):
        sum_half(m, 0)
    scale_copy.wait_recv()

    for applied in range(2):
        if applied:
            for m in range(ne):
                send_all(m, True)
            for m in range(ne):
                sum_half(m, 1)
        for m in range(ne):
            answer_all(m, applied)
        for m in range(ne):
            gather_rows(m)
        if not applied:
            repeat(0, blocks // unit, scale_again)

    def fin_copy(j):
        return to_edge(
            fin_send.at[j], fin_recv.at[e], fin_send_sem.at[j], fin_recv_sem.at[e], edge_at(j)
        )

    for j in range(ne - 1, -1, -1):
        for k in range(share):
            b = edge_at(j) * share + k
            value = (rs[pl.ds(b, 1), :] * acc[last[b]]).astype(BF16)
            if j:
                fin_send[j, k] = value
            else:
                fin_recv[e, k] = value
        if j:
            fin_copy(j).start()
    for j in range(1, ne):
        source = edge_at(j)
        to_edge(
            fin_send.at[0], fin_recv.at[source], fin_send_sem.at[0], fin_recv_sem.at[source], e
        ).wait_recv()
    for k in range(share):
        for g in range(ne // group):
            stacked = jnp.concatenate(
                [
                    fin_recv[g * group + i, k].astype(F32)
                    for i in range(group)
                ],
                axis=0,
            )
            out[pl.ds(k * block, block), pl.ds(g * LANES, LANES)] = stacked.T.astype(BF16)

    for copy in meta_copies + tile_copies + relays:
        copy.wait_send()
    repeat(1, half, lambda t: mv_copy(t).wait_send())
    scale_copy.wait_send()
    for m in range(ne):
        for applied in range(2):
            mir_copy(applied * ne + m).wait_send()
        repeat(1, half, lambda t: fwd_copy(m, t).wait_send())
        repeat(1, half, lambda t: bwd_copy(m, t).wait_send())
    for j in range(1, ne):
        fin_copy(j).wait_send()


def shards(
    features, incidence, send_count, row_block, edge_block, edge_weight, edge_degree, vertex_degree
):
    nv = lax.axis_size("vert")
    ne = lax.axis_size("edge")
    papers, width = features.shape
    slots, block, _ = incidence.shape
    blocks = papers // block
    hyper_blocks = edge_weight.shape[0]
    cols = width // ne
    share = blocks // ne
    half = nv // 2
    scratch = [
        ((papers, LANES), F32),
        ((hyper_blocks, block), F32),
        ((hyper_blocks, block), jnp.int32),
        ((blocks, block), jnp.int32),
        ((ne, slots, block, block), BF16),
        ((ne, 8, LANES), jnp.int32),
        ((ne, 8, LANES), F32),
        ((ne, 8, LANES), F32),
        ((half, 8, LANES), jnp.int32),
        None,
        None,
        ((blocks, cols, block), BF16),
        ((blocks, block), F32),
        ((ne, half, 2, cols, block), BF16),
        ((ne, half, 2, cols, block), BF16),
        ((ne, half, 2, cols, block), BF16),
        ((ne, half, 2, cols, block), BF16),
        ((nv * ne + 1, cols, block), F32),
        None,
        None,
        ((ne, 2, hyper_blocks, cols, block), F32),
        ((2, hyper_blocks, cols, block), BF16),
        ((2 * ne, 2, hyper_blocks, cols, block), BF16),
        ((2 * ne, 2, hyper_blocks, cols, block), BF16),
        ((ne, share, cols, block), BF16),
        ((ne, share, cols, block), BF16),
    ]
    scalars = iter(
        [(ne, 8, LANES), (half, 8, LANES), (nv * ne,), (blocks,)]
    )
    held = sum(
        math.prod(item[0]) * jnp.dtype(item[1]).itemsize for item in scratch if item is not None
    )
    held += papers // ne * width * 2
    shapes = [
        pltpu.SMEM(next(scalars), jnp.int32) if item is None else pltpu.VMEM(*item)
        for item in scratch
    ]
    dma = pltpu.SemaphoreType.DMA
    sems = [dma((ne,))] * 4 + [dma((2, ne))] * 3 + [dma((half,))] * 2 + [dma((ne, half))] * 4
    sems += [dma((ne,))] * 2 + [dma((2 * ne + 1,))] * 2 + [dma((7,))]
    hbm = pl.BlockSpec(memory_space=pltpu.HBM)
    vmem = pl.BlockSpec(memory_space=pltpu.VMEM)
    smem = pl.BlockSpec(memory_space=pltpu.SMEM)
    return pl.pallas_call(
        functools.partial(kernel, nv, ne),
        out_shape=jax.ShapeDtypeStruct((papers // ne, width), BF16),
        in_specs=[hbm, hbm, smem, smem, smem, hbm, hbm, hbm],
        out_specs=vmem,
        scratch_shapes=shapes + sems,
        compiler_params=pltpu.CompilerParams(
            collective_id=0,
            has_side_effects=True,
            vmem_limit_bytes=max(held + 6 * 2**20, 60 * 2**20),
        ),
        cost_estimate=pl.CostEstimate(
            flops=8 * slots * ne * block * block * cols,
            bytes_accessed=features.size * 4 + incidence.size * 2,
            transcendentals=0,
        ),
    )(
        features,
        incidence,
        send_count.reshape(1, slots),
        row_block.reshape(1, slots),
        edge_block.reshape(1, slots),
        edge_weight,
        edge_degree,
        vertex_degree.reshape(blocks, block),
    ).astype(F32)


def solution(mesh):
    placed = (
        P("vert", None),
        P("vert", None, "edge"),
        P("vert", "edge"),
        P("vert", "edge"),
        P("vert", "edge"),
        P("vert", "edge"),
        P("vert", "edge"),
        P("vert"),
    )
    return jax.shard_map(
        shards, mesh=mesh, in_specs=placed, out_specs=P(("vert", "edge"), None), check_vma=False
    )
```

```python
import functools
import math

import jax
import jax.numpy as jnp
from jax import lax
from jax.experimental import pallas as pl
from jax.experimental.pallas import tpu as pltpu
from jax.sharding import PartitionSpec as P

MESH = pl.DeviceIdType.MESH
LANES = 128
BF16 = jnp.bfloat16
F32 = jnp.float32


def repeat(start, stop, body):
    if stop - start <= 3:
        for step in range(start, stop):
            body(step)
    else:

        @pl.loop(start, stop)
        def _(step):
            body(step)


def kernel(
    nv,
    ne,
    feat,
    inc,
    live_s,
    row_s,
    edge_s,
    weight,
    degree,
    vdeg,
    out,
    mine,
    weight_v,
    degree_v,
    vdeg_v,
    tiles,
    meta_e,
    scale_e,
    scale_m,
    meta_v,
    keys,
    owner_blocks,
    xs,
    rs,
    fwd_send,
    fwd_recv,
    bwd_send,
    bwd_recv,
    acc,
    prev,
    last,
    hyper_acc,
    hyper_feat,
    mir_send,
    mir_recv,
    fin_send,
    fin_recv,
    meta_send_sem,
    meta_recv_sem,
    scale_send_sem,
    scale_recv_sem,
    tile_send_sem,
    tile_recv_sem,
    relay_sem,
    mv_send_sem,
    mv_recv_sem,
    fwd_send_sem,
    fwd_recv_sem,
    bwd_send_sem,
    bwd_recv_sem,
    fin_send_sem,
    fin_recv_sem,
    mir_send_sem,
    mir_recv_sem,
    local_sem,
):
    v = lax.axis_index("vert")
    e = lax.axis_index("edge")
    block = inc.shape[1]
    blocks = xs.shape[0]
    cols = xs.shape[1]
    hyper_blocks = weight.shape[0]
    share = blocks // ne
    none = nv * ne
    half = nv // 2
    here = v % half
    base = v - here
    mirror = (v + half) % nv
    sibling = e + 1 - 2 * (e % 2)

    def edge_at(j):
        first = e + (j % 2) * (sibling - e)
        return (first + 2 * (j // 2)) % ne

    def ahead(t):
        return base + (here + t) % half

    def behind(t):
        return (here - t + half) % half

    def to_edge(src, dst, send_sem, recv_sem, target):
        return pltpu.make_async_remote_copy(
            src_ref=src,
            dst_ref=dst,
            send_sem=send_sem,
            recv_sem=recv_sem,
            device_id=(v, target),
            device_id_type=MESH,
        )

    def to_vert(src, dst, send_sem, recv_sem, target):
        return pltpu.make_async_remote_copy(
            src_ref=src,
            dst_ref=dst,
            send_sem=send_sem,
            recv_sem=recv_sem,
            device_id=(target, e),
            device_id_type=MESH,
        )

    group = LANES // cols
    start = pl.multiple_of((e // group) * LANES, LANES)
    part = e % group
    fetches = [
        pltpu.make_async_copy(weight, weight_v, local_sem.at[2]),
        pltpu.make_async_copy(degree, degree_v, local_sem.at[3]),
        pltpu.make_async_copy(vdeg, vdeg_v, local_sem.at[4]),
        pltpu.make_async_copy(feat.at[:, pl.ds(start, LANES)], mine, local_sem.at[5]),
        pltpu.make_async_copy(inc, tiles.at[e], local_sem.at[6]),
    ]
    for copy in fetches:
        copy.start()

    barrier = pltpu.get_barrier_semaphore()

    def greet_vert(t):
        pl.semaphore_signal(barrier, inc=1, device_id=(ahead(t), e), device_id_type=MESH)

    repeat(1, half, greet_vert)
    pl.semaphore_signal(barrier, inc=1, device_id=(mirror, e), device_id_type=MESH)
    for j in range(1, ne):
        pl.semaphore_signal(barrier, inc=1, device_id=(v, edge_at(j)), device_id_type=MESH)

    lane = lax.broadcasted_iota(jnp.int32, (8, LANES), 1)
    sub = lax.broadcasted_iota(jnp.int32, (8, LANES), 0)
    packed = jnp.zeros((8, LANES), jnp.int32)
    for s in range(nv):
        key = jnp.where(live_s[0, s] > 0, row_s[0, s], -1)
        both = jnp.where(sub == 0, key, edge_s[0, s])
        packed = jnp.where(lane == s, both, packed)
    meta_e[e] = packed
    for copy in fetches[:2]:
        copy.wait()
    scale_e[e, :hyper_blocks] = weight_v[...] / jnp.maximum(degree_v[...], 1).astype(F32)

    pl.semaphore_wait(barrier, half + ne - 1)

    meta_copies, tile_copies = [], []
    for j in range(1, ne):
        target = edge_at(j)
        meta_copies.append(
            to_edge(
                meta_e.at[e], meta_e.at[e], meta_send_sem.at[j], meta_recv_sem.at[e], target
            )
        )
        meta_copies.append(
            to_edge(
                scale_e.at[e], scale_e.at[e], scale_send_sem.at[j], scale_recv_sem.at[e], target
            )
        )
    for copy in meta_copies:
        copy.start()
    for j in [1] + list(range(2, ne, 2)):
        for q in range(2):
            some = pl.ds(q * half, half)
            copy = to_edge(
                inc.at[some],
                tiles.at[e, some],
                tile_send_sem.at[q, j],
                tile_recv_sem.at[q, e],
                edge_at(j),
            )
            copy.start()
            tile_copies.append(copy)

    for copy in fetches[2:4]:
        copy.wait()
    rs[...] = 1.0 / jnp.sqrt(jnp.maximum(vdeg_v[...], 1).astype(F32))
    unit = math.gcd(blocks, 4)

    def prepare(u):
        for i in range(unit):
            b = u * unit + i
            turned = mine[pl.ds(pl.multiple_of(b * block, block), block), :].T
            picked = turned[:cols]
            for g in range(1, group):
                picked = jnp.where(part == g, turned[g * cols : (g + 1) * cols], picked)
            picked = (picked * rs[pl.ds(b, 1), :]).astype(BF16)
            xs[b] = picked

    repeat(0, blocks // unit, prepare)
    fetches[4].wait()

    def partial(other, s):
        key = keys[other, 0, s]
        value = jnp.dot(
            xs[jnp.maximum(key, 0)], tiles[other, s], preferred_element_type=F32
        )
        return jnp.where(key >= 0, value, 0.0).astype(BF16)

    def fwd_copy(c, t):
        return to_vert(
            fwd_send.at[c, t],
            fwd_recv.at[c, here],
            fwd_send_sem.at[c, t],
            fwd_recv_sem.at[c, here],
            ahead(t),
        )

    def fwd_arrival(c, source):
        return to_vert(
            fwd_send.at[c, 0],
            fwd_recv.at[c, source],
            fwd_send_sem.at[c, 0],
            fwd_recv_sem.at[c, source],
            v,
        )

    def bwd_copy(c, t):
        return to_vert(
            bwd_send.at[c, t],
            bwd_recv.at[c, here],
            bwd_send_sem.at[c, t],
            bwd_recv_sem.at[c, here],
            ahead(t),
        )

    def bwd_arrival(c, source):
        return to_vert(
            bwd_send.at[c, 0],
            bwd_recv.at[c, source],
            bwd_send_sem.at[c, 0],
            bwd_recv_sem.at[c, source],
            v,
        )

    def mv_copy(t):
        return to_vert(
            meta_v.at[here], meta_v.at[here], mv_send_sem.at[t], mv_recv_sem.at[here], ahead(t)
        )

    def mv_arrival(source):
        return to_vert(
            meta_v.at[here], meta_v.at[source], mv_send_sem.at[0], mv_recv_sem.at[source], v
        )

    def tile_arrival(q, source):
        some = pl.ds(q * half, half)
        return to_edge(
            inc.at[some],
            tiles.at[source, some],
            tile_send_sem.at[q, 0],
            tile_recv_sem.at[q, source],
            e,
        )

    def mir_copy(p):
        return to_vert(
            mir_send.at[p], mir_recv.at[p], mir_send_sem.at[p], mir_recv_sem.at[p], mirror
        )

    scale_copy = to_vert(
        scale_e, scale_m, mir_send_sem.at[2 * ne], mir_recv_sem.at[2 * ne], mirror
    )

    for j in range(1, ne):
        source = edge_at(j)
        to_edge(
            meta_e.at[e], meta_e.at[source], meta_send_sem.at[0], meta_recv_sem.at[source], e
        ).wait_recv()
        to_edge(
            scale_e.at[e], scale_e.at[source], scale_send_sem.at[0], scale_recv_sem.at[source], e
        ).wait_recv()
    to_scalars = pltpu.make_async_copy(meta_e, keys, local_sem.at[0])
    to_scalars.start()
    seen = jnp.zeros((8, LANES), jnp.int32)
    for other in range(ne):
        seen = jnp.where(sub == other, meta_e[other, 1:2, :], seen)
    meta_v[here] = seen
    repeat(1, half, lambda t: mv_copy(t).start())
    scale_copy.start()
    to_scalars.wait()

    relays = []
    def relay(j, q):
        source = edge_at(j)
        some = pl.ds(q * half, half)
        tile_arrival(q, source).wait_recv()
        if j >= 2 and j % 2 == 0:
            copy = to_edge(
                tiles.at[source, some],
                tiles.at[source, some],
                relay_sem.at[q, j],
                tile_recv_sem.at[q, source],
                sibling,
            )
            copy.start()
            relays.append(copy)

    def send_all(m, again=False):
        def step(t):
            if again:
                fwd_copy(m, t).wait_send()
            for q in range(2):
                fwd_send[m, t, q] = partial(edge_at(m), q * half + (here + t) % half)
            fwd_copy(m, t).start()

        repeat(1, half, step)
        for q in range(2):
            fwd_recv[m, here, q] = partial(edge_at(m), q * half + here)

    def sum_half(m, applied):
        def add_from(source, first):
            for q in range(2):
                held = owner_blocks[source, edge_at(m), q * half + here]
                value = fwd_recv[m, source, q].astype(F32)
                for h in range(hyper_blocks):
                    term = jnp.where(held == h, value, 0.0)
                    if not first:
                        term = hyper_acc[m, q, h] + term
                    hyper_acc[m, q, h] = term

        add_from(here, True)

        def arrive(t):
            fwd_arrival(m, behind(t)).wait_recv()
            add_from(behind(t), False)

        repeat(1, half, arrive)
        mir_send[applied * ne + m] = hyper_acc[m].astype(BF16)
        mir_copy(applied * ne + m).start()

    def answer_all(m, applied):
        p = applied * ne + m
        mir_copy(p).wait_recv()
        for q in range(2):
            own = q == v // half
            scale = jnp.where(own, scale_e[edge_at(m)], scale_m[edge_at(m)])
            for h in range(hyper_blocks):
                total = hyper_acc[m, q, h] + mir_recv[p, q, h].astype(F32)
                hyper_feat[q, h] = (total * scale[h : h + 1, :]).astype(BF16)

        def answer(t):
            if applied:
                bwd_copy(m, t).wait_send()
            for q in range(2):
                held = owner_blocks[(here + t) % half, edge_at(m), q * half + here]
                bwd_send[m, t, q] = hyper_feat[q, held]
            bwd_copy(m, t).start()

        repeat(1, half, answer)
        for q in range(2):
            held = owner_blocks[here, edge_at(m), q * half + here]
            bwd_recv[m, here, q] = hyper_feat[q, held]

    def gather_rows(m):
        def spread(t):
            values = [
                lax.dot_general(
                    bwd_recv[m, behind(t), q],
                    tiles[edge_at(m), q * half + behind(t)],
                    (((1,), (1,)), ((), ())),
                    preferred_element_type=F32,
                )
                for q in range(2)
            ]
            for n, value in enumerate(values):
                i = (m * half + t) * 2 + n
                acc[i] = value + acc[prev[i]]

        spread(0)

        def come_back(t):
            bwd_arrival(m, behind(t)).wait_recv()
            spread(t)

        repeat(1, half, come_back)

    def scale_again(u):
        for i in range(unit):
            b = u * unit + i
            scale = rs[pl.ds(b, 1), :]
            xs[b] = (scale * (scale * acc[last[b]])).astype(BF16)

    send_all(0)
    for q in range(2):
        relay(1, q)
    send_all(1)
    def link(i, latest):
        other = edge_at(i // (2 * half))
        slot = (i % 2) * half + behind((i // 2) % half)
        key = keys[other, 0, slot]
        before = none
        for b in range(blocks):
            before = jnp.where(key == b, latest[b], before)
        prev[i] = before
        return tuple(jnp.where(key == b, i, latest[b]) for b in range(blocks))

    latest = lax.fori_loop(0, none, link, (jnp.int32(none),) * blocks)
    for b in range(blocks):
        last[b] = latest[b]
    acc[none] = jnp.zeros(acc.shape[1:], F32)

    repeat(1, half, lambda t: mv_arrival(behind(t)).wait_recv())
    to_scalars = pltpu.make_async_copy(meta_v, owner_blocks, local_sem.at[1])
    to_scalars.start()
    to_scalars.wait()

    for m in range(2, ne):
        sum_half(m - 2, 0)
        for q in range(2):
            relay(m, q)
        send_all(m)
    for m in range(ne - 2, ne):
        sum_half(m, 0)
    scale_copy.wait_recv()

    for applied in range(2):
        if applied:
            for m in range(ne):
                send_all(m, True)
            for m in range(ne):
                sum_half(m, 1)
        for m in range(ne):
            answer_all(m, applied)
            if m >= 2:
                gather_rows(m - 2)
        for m in range(ne - 2, ne):
            gather_rows(m)
        if not applied:
            repeat(0, blocks // unit, scale_again)

    def fin_copy(j):
        return to_edge(
            fin_send.at[j], fin_recv.at[e], fin_send_sem.at[j], fin_recv_sem.at[e], edge_at(j)
        )

    for j in range(ne - 1, -1, -1):
        for k in range(share):
            b = edge_at(j) * share + k
            value = (rs[pl.ds(b, 1), :] * acc[last[b]]).astype(BF16)
            if j:
                fin_send[j, k] = value
            else:
                fin_recv[e, k] = value
        if j:
            fin_copy(j).start()
    for j in range(1, ne):
        source = edge_at(j)
        to_edge(
            fin_send.at[0], fin_recv.at[source], fin_send_sem.at[0], fin_recv_sem.at[source], e
        ).wait_recv()
    for k in range(share):
        for g in range(ne // group):
            stacked = jnp.concatenate(
                [
                    fin_recv[g * group + i, k].astype(F32)
                    for i in range(group)
                ],
                axis=0,
            )
            out[pl.ds(k * block, block), pl.ds(g * LANES, LANES)] = stacked.T.astype(BF16)

    for copy in meta_copies + tile_copies + relays:
        copy.wait_send()
    repeat(1, half, lambda t: mv_copy(t).wait_send())
    scale_copy.wait_send()
    for m in range(ne):
        for applied in range(2):
            mir_copy(applied * ne + m).wait_send()
        repeat(1, half, lambda t: fwd_copy(m, t).wait_send())
        repeat(1, half, lambda t: bwd_copy(m, t).wait_send())
    for j in range(1, ne):
        fin_copy(j).wait_send()


def shards(
    features, incidence, send_count, row_block, edge_block, edge_weight, edge_degree, vertex_degree
):
    nv = lax.axis_size("vert")
    ne = lax.axis_size("edge")
    papers, width = features.shape
    slots, block, _ = incidence.shape
    blocks = papers // block
    hyper_blocks = edge_weight.shape[0]
    cols = width // ne
    share = blocks // ne
    half = nv // 2
    scratch = [
        ((papers, LANES), F32),
        ((hyper_blocks, block), F32),
        ((hyper_blocks, block), jnp.int32),
        ((blocks, block), jnp.int32),
        ((ne, slots, block, block), BF16),
        ((ne, 8, LANES), jnp.int32),
        ((ne, 8, LANES), F32),
        ((ne, 8, LANES), F32),
        ((half, 8, LANES), jnp.int32),
        None,
        None,
        ((blocks, cols, block), BF16),
        ((blocks, block), F32),
        ((ne, half, 2, cols, block), BF16),
        ((ne, half, 2, cols, block), BF16),
        ((ne, half, 2, cols, block), BF16),
        ((ne, half, 2, cols, block), BF16),
        ((nv * ne + 1, cols, block), F32),
        None,
        None,
        ((ne, 2, hyper_blocks, cols, block), F32),
        ((2, hyper_blocks, cols, block), BF16),
        ((2 * ne, 2, hyper_blocks, cols, block), BF16),
        ((2 * ne, 2, hyper_blocks, cols, block), BF16),
        ((ne, share, cols, block), BF16),
        ((ne, share, cols, block), BF16),
    ]
    scalars = iter(
        [(ne, 8, LANES), (half, 8, LANES), (nv * ne,), (blocks,)]
    )
    held = sum(
        math.prod(item[0]) * jnp.dtype(item[1]).itemsize for item in scratch if item is not None
    )
    held += papers // ne * width * 2
    shapes = [
        pltpu.SMEM(next(scalars), jnp.int32) if item is None else pltpu.VMEM(*item)
        for item in scratch
    ]
    dma = pltpu.SemaphoreType.DMA
    sems = [dma((ne,))] * 4 + [dma((2, ne))] * 3 + [dma((half,))] * 2 + [dma((ne, half))] * 4
    sems += [dma((ne,))] * 2 + [dma((2 * ne + 1,))] * 2 + [dma((7,))]
    hbm = pl.BlockSpec(memory_space=pltpu.HBM)
    vmem = pl.BlockSpec(memory_space=pltpu.VMEM)
    smem = pl.BlockSpec(memory_space=pltpu.SMEM)
    return pl.pallas_call(
        functools.partial(kernel, nv, ne),
        out_shape=jax.ShapeDtypeStruct((papers // ne, width), BF16),
        in_specs=[hbm, hbm, smem, smem, smem, hbm, hbm, hbm],
        out_specs=vmem,
        scratch_shapes=shapes + sems,
        compiler_params=pltpu.CompilerParams(
            collective_id=0,
            has_side_effects=True,
            vmem_limit_bytes=max(held + 6 * 2**20, 60 * 2**20),
        ),
        cost_estimate=pl.CostEstimate(
            flops=8 * slots * ne * block * block * cols,
            bytes_accessed=features.size * 4 + incidence.size * 2,
            transcendentals=0,
        ),
    )(
        features,
        incidence,
        send_count.reshape(1, slots),
        row_block.reshape(1, slots),
        edge_block.reshape(1, slots),
        edge_weight,
        edge_degree,
        vertex_degree.reshape(blocks, block),
    ).astype(F32)


def solution(mesh):
    placed = (
        P("vert", None),
        P("vert", None, "edge"),
        P("vert", "edge"),
        P("vert", "edge"),
        P("vert", "edge"),
        P("vert", "edge"),
        P("vert", "edge"),
        P("vert"),
    )
    return jax.shard_map(
        shards, mesh=mesh, in_specs=placed, out_specs=P(("vert", "edge"), None), check_vma=False
    )
```
